128 devices in a mesh: near: 4 (over z), brick: 32 (over x, y, core).
Axes of the slice: x: 4, y: 4, z: 4, core: 2. Of those that a mesh axis runs over, the one named last changes fastest.
Arguments:
- recv_pos: float32 [3, 4194304], P(None, ('near', 'brick')), may hold values from -0.4 to 0.4
- donor_cell: int32 [4194304], P(('near', 'brick')), may hold values from 0 to 16383
- block_owner: int32 [32768, 1], P(('near', 'brick')), may hold values from 0 to 127; in each aligned block of 256 rows (0 to 255, 256 to 511, ...) at most 4 rows name the same one
- cell_geom: float32 [24, 2097152], P(None, ('near', 'brick')), may hold values from -0.68 to 0.68, as said below
- cell_values: float32 [40, 2097152], P(None, ('near', 'brick')), may hold values from -6 to 6
Outputs:
- fringe: float32 [5, 4194304], P(None, ('near', 'brick'))
The draws below stay inside these ranges and needn't reach their ends.
Inputs may be any that keep to these rules, and one draw needn't show every extreme that they name: `block_owner`: in the 256 blocks of one device no owner is named more than 4 times, a bound that some block reaches; owners index the devices in mesh order, near slowest. `cell_geom`: row c * 8 + v is s_c(v) / 2 plus a term of magnitude at most 0.18.
All inputs are finite; a program needn't handle non-finite values.
Results may differ from the reference program's by a relative error of at most 0.0001.
Values sent between devices are 32-bit elements; how exact they have to be, the bound alone decides.
No kernel may reach another device: no remote copies, remote signals or barrier semaphores. Data moves between devices by JAX's collectives and lax.ppermute only.
A program may use at most 192 MiB of HBM per device.

```python
import math
import jax
import jax.numpy as jnp
import numpy as np
from jax import lax

BLOCK = 128
CAP = 4
NB = 256
CELLS = 16384
NEWTON = 3
VARS = 5
NB_ALL = 32768
RECEPTORS = 4194304
CELLS_ALL = 2097152
DEVICES = 128


def draw_cell_geom(key, part):
    key = jax.random.fold_in(key, 11)
    key_size = jax.random.fold_in(key, 1)
    key_sign = jax.random.fold_in(key, 2)
    key_noise = jax.random.fold_in(key, 3)
    rows = jnp.arange(24, dtype=jnp.int32)
    vertex = rows % 8
    coord = rows // 8
    sign_zero = 2 * (vertex % 2) - 1
    sign_one = 2 * (vertex // 2 % 2) - 1
    sign_two = 2 * (vertex // 4 % 2) - 1
    own_sign = 2 * (vertex // 2 ** coord % 2) - 1
    others = (sign_zero * sign_one * sign_two * own_sign).astype(jnp.float32)[:, None]
    nominal = (0.5 * own_sign.astype(jnp.float32))[:, None]
    strength = jax.random.uniform(key_size, (3, CELLS_ALL), jnp.float32, 0.15, 0.3)
    jitter = jax.random.uniform(key_noise, (24, CELLS_ALL), jnp.float32, -0.03, 0.03)
    flips = jax.random.bernoulli(key_sign, 0.5, (3, CELLS_ALL))
    twist = jnp.where(flips, strength, -strength)
    twist_rows = jnp.repeat(twist, 8, axis=0)
    return nominal + 0.5 * twist_rows * others + jitter


def touch_ends(entries, key, least, high):
    shape = entries.shape
    place = [jax.random.randint(jax.random.fold_in(key, axis), (), 0, shape[axis]) for axis in range(len(shape))]
    entries = entries.at[tuple(place)].set(least)
    longest = shape.index(max(shape))
    place[longest] = (place[longest] + 1) % shape[longest]
    return entries.at[tuple(place)].set(high)


def shard_levels(key, shape, pieces, low, largest):
    gain, own = 1.0, jax.random.fold_in(key, 6)
    for dim, blocks in pieces:
        heights = jnp.exp(jax.random.uniform(jax.random.fold_in(own, dim), (blocks,), jnp.float32, low / len(pieces), largest / len(pieces)))
        gain = gain * jnp.repeat(heights, shape[dim] // blocks).reshape([-1 if axis == dim else 1 for axis in range(len(shape))])
    return gain


def routed_block(key, own, number, rows, count, top, limit, slope):
    sequence = jax.random.permutation(key, count)
    packed, common = load_shares(count, rows * top, limit, slope, True), load_shares(count, rows * top, limit, slope, False)
    places = jnp.arange(count)

    def named(tallies, turn):
        used = int((tallies > 0).sum())
        fixed = max(1, used // 4)
        shifted = fixed + (places - fixed + turn * (used - fixed)) % max(1, count - fixed)
        return jnp.zeros((count,), jnp.int32).at[sequence[jnp.where(places < fixed, places, shifted)]].set(jnp.asarray(tallies, jnp.int32))

    tallies = jnp.where(number % 4 == 0, named(packed, number // 4), named(common, number - number // 4 - 1))
    mixed = jax.random.permutation(jax.random.fold_in(own, 3), count)
    giver, taker = mixed[0:count // 2 * 2:2], mixed[1:count // 2 * 2:2]
    slack = jnp.minimum(tallies[giver] - 1, limit - tallies[taker]) // 2
    slack = jnp.where((giver == sequence[0]) | (taker == sequence[0]) | (tallies[taker] == 0), 0, jnp.maximum(slack, 0))
    shifted = jax.random.randint(jax.random.fold_in(own, 4), (count // 2,), 0, 1 << 20) % (slack + 1)
    tallies = tallies.at[giver].add(-shifted).at[taker].add(shifted)
    labels = jnp.searchsorted(jnp.cumsum(tallies), jnp.arange(rows * top), side="right").astype(jnp.int32)
    listing = labels.reshape(top, rows).T
    listing = listing[jax.random.permutation(jax.random.fold_in(own, 1), rows)]
    turn = jax.random.randint(jax.random.fold_in(own, 2), (rows, 1), 0, top)
    return jnp.take_along_axis(listing, (jnp.arange(top)[None, :] + turn) % top, axis=1)


def load_shares(count, total, reach, slope, full):
    weights = [(1 << 20) // math.isqrt(standing ** slope) + 1 for standing in range(1, count + 1)]
    largest = reach if full else min(reach, max(-(-total // count), total * weights[0] // sum(weights)))
    least = 1 if total - largest >= count - 1 else 0
    counts, rest = [largest] + [least] * (count - 1), total - largest - least * (count - 1)
    while rest > 0:
        free = [i for i in range(1, count) if counts[i] < largest] or [i for i in range(1, count) if counts[i] < reach]
        pool, remaining = sum([weights[i] for i in free]), rest
        for i in free:
            addition = min(reach - counts[i], max(1, remaining * weights[i] // pool), rest)
            counts[i] = counts[i] + addition
            rest = rest - addition
    return np.array(counts)


def centred(own_key, dims, scale, reach, split=(), kind=jnp.bfloat16):
    gain = shard_levels(own_key, dims, split, -0.22, 0.18) if split else 1.0
    values = jax.random.normal(own_key, dims, jnp.float32) * scale * gain
    return jnp.minimum(jnp.maximum(values, -reach), reach).astype(kind)


def setup_inputs(seed: int = 0) -> dict:
    seeds = jax.random.split(jax.random.key(seed), 6)
    recv_pos = jnp.clip(jax.random.uniform(seeds[0], (3, RECEPTORS), jnp.float32, -0.4, 0.4) * shard_levels(seeds[0], (3, RECEPTORS), ((1, 128),), -0.4, 0.0), -0.4, 0.4)
    donor_cell = touch_ends(jax.random.randint(seeds[1], (RECEPTORS,), 0, CELLS), jax.random.fold_in(seeds[1], 1), 0, CELLS - 1).astype(jnp.int32)
    block_owner_keys = jax.random.split(jax.random.fold_in(seeds[2], 1), NB_ALL // NB)
    block_owner_turns = jax.random.permutation(jax.random.fold_in(seeds[2], 3), NB_ALL // NB)
    block_owner = jax.vmap(lambda own, number: routed_block(jax.random.fold_in(seeds[2], 2), own, number, NB, DEVICES, 1, CAP, 2))(block_owner_keys, block_owner_turns).reshape((NB_ALL, 1))
    cell_geom = draw_cell_geom(jax.random.fold_in(seeds[5], 71), 0)
    cell_values = centred(seeds[4], (40, CELLS_ALL), 1.0, 6.0, ((1, 128),), jnp.float32)
    return {"recv_pos": recv_pos, "donor_cell": donor_cell, "block_owner": block_owner, "cell_geom": cell_geom, "cell_values": cell_values}


corner_signs = np.array([[2 * (v % 2) - 1 for v in range(8)], [2 * ((v // 2) % 2) - 1 for v in range(8)], [2 * ((v // 4) % 2) - 1 for v in range(8)]], dtype=np.float32)


def shape_weights(coords):
    signs = jnp.asarray(corner_signs, jnp.float32)
    linear = 0.5 * (1.0 + signs[:, :, None] * coords[:, None, :])
    weights = linear[0] * linear[1] * linear[2]
    half = 0.5 * signs[:, :, None]
    slopes = (half[0] * linear[1] * linear[2], linear[0] * half[1] * linear[2], linear[0] * linear[1] * half[2])
    return weights, slopes


def det_three(col_a, col_b, col_c):
    cross_x = col_b[1] * col_c[2] - col_b[2] * col_c[1]
    cross_y = col_b[2] * col_c[0] - col_b[0] * col_c[2]
    cross_z = col_b[0] * col_c[1] - col_b[1] * col_c[0]
    return col_a[0] * cross_x + col_a[1] * cross_y + col_a[2] * cross_z


def interpolate(geometry, values, position):
    coords = jnp.zeros_like(position)
    for step in range(NEWTON):
        weights, slopes = shape_weights(coords)
        misfit = jnp.sum(geometry * weights[None], axis=1) - position
        col_a = jnp.sum(geometry * slopes[0][None], axis=1)
        col_b = jnp.sum(geometry * slopes[1][None], axis=1)
        col_c = jnp.sum(geometry * slopes[2][None], axis=1)
        determ = det_three(col_a, col_b, col_c)
        delta = jnp.stack([det_three(misfit, col_b, col_c), det_three(col_a, misfit, col_c), det_three(col_a, col_b, misfit)]) / determ
        coords = coords - delta
    weights, slopes = shape_weights(coords)
    return jnp.sum(values * weights[None], axis=1)


def reference(recv_pos, donor_cell, block_owner, cell_geom, cell_values):
    owners = jnp.repeat(block_owner[:, 0], BLOCK)
    global_cell = (owners * CELLS + donor_cell).astype(jnp.int32)
    rows_dev = NB * BLOCK
    pos_parts = recv_pos.reshape(3, DEVICES, rows_dev).transpose(1, 0, 2)
    cell_parts = global_cell.reshape(DEVICES, rows_dev)

    def one_part(pair):
        position, cells = pair
        count = cells.shape[0]
        geometry = jnp.take(cell_geom, cells, axis=1).reshape(3, 8, count)
        values = jnp.take(cell_values, cells, axis=1).reshape(VARS, 8, count)
        return interpolate(geometry, values, position)

    result = lax.map(one_part, (pos_parts, cell_parts))
    return result.transpose(1, 0, 2).reshape(VARS, RECEPTORS)
```

```python
import functools

import jax
import jax.numpy as jnp
import numpy as np
from jax import lax
from jax.experimental import pallas as pl
from jax.experimental.pallas import tpu as pltpu
from jax.sharding import PartitionSpec as P

BLOCK = 128
CAP = 4
NEWTON = 3
VARS = 5
FIELDS = 64
AXES = ("near", "brick")
NT = (((1,), (1,)), ((), ()))


def monomial_matrix():
    signs = np.array([[2 * (v >> d & 1) - 1 for v in range(8)] for d in range(3)])
    rows = [np.ones(8), signs[0], signs[1], signs[2]]
    rows += [signs[0] * signs[1], signs[0] * signs[2], signs[1] * signs[2]]
    rows += [signs[0] * signs[1] * signs[2]]
    block = np.stack(rows) / 8.0
    full = np.kron(np.eye(FIELDS // 8), block)
    return np.concatenate([full, full], axis=1).astype(np.float32)


def pack_kernel(cells_per, turn_ref, owner_ref, pos_ref, cell_ref, out_ref, place_ref, spot, lists, sem):
    blocks = owner_ref.shape[1]
    owner = owner_ref[...]
    key = jnp.broadcast_to((owner >> 1).astype(jnp.float32), (blocks, blocks))
    earlier = lax.broadcasted_iota(jnp.int32, (blocks, blocks), 0)
    later = lax.broadcasted_iota(jnp.int32, (blocks, blocks), 1)
    same = jnp.where((key.T == key) & (earlier < later), 1.0, 0.0)
    rank = jnp.sum(same, axis=0, keepdims=True).astype(jnp.int32)
    core = (rank + turn_ref[0]) & 1
    place = ((owner & -2) + core) * CAP + (rank >> 1)
    place_ref[...] = place
    spot[0:1, :] = place
    spot[1:2, :] = ((owner ^ core) & 1) * cells_per
    copy = pltpu.make_async_copy(spot, lists, sem)
    copy.start()
    out_ref[...] = jnp.full(out_ref.shape, -1.0, jnp.float32)
    copy.wait()

    def one(b, carry):
        at = pl.multiple_of(b * BLOCK, BLOCK)
        e = lists[0, b]
        out_ref[e, 0:3, :] = pos_ref[:, pl.ds(at, BLOCK)]
        out_ref[e, 3:4, :] = (cell_ref[pl.ds(b, 1), :] + lists[1, b]).astype(jnp.float32)
        return carry

    lax.fori_loop(0, blocks, one, 0, unroll=8)


def pack(turn, owner, pos, cell, cells_per, slots):
    blocks = owner.shape[1]
    return pl.pallas_call(
        functools.partial(pack_kernel, cells_per),
        name="pack",
        in_specs=[pl.BlockSpec(memory_space=pltpu.SMEM)] + [pl.BlockSpec(memory_space=pltpu.VMEM)] * 3,
        out_specs=[pl.BlockSpec(memory_space=pltpu.VMEM)] * 2,
        out_shape=[
            jax.ShapeDtypeStruct((slots, 4, BLOCK), jnp.float32),
            jax.ShapeDtypeStruct((1, blocks), jnp.int32),
        ],
        scratch_shapes=[
            pltpu.VMEM((2, blocks), jnp.int32),
            pltpu.SMEM((2, blocks), jnp.int32),
            pltpu.SemaphoreType.DMA,
        ],
        compiler_params=pltpu.CompilerParams(vmem_limit_bytes=8 << 20),
    )(turn, owner, pos, cell)


CHUNK = 2048
TILE = 256


def table_kernel(steps, geom_ref, vals_ref, geom_two, vals_two, out_ref):
    row = lax.broadcasted_iota(jnp.int32, (TILE, TILE), 0)
    col = lax.broadcasted_iota(jnp.int32, (TILE, TILE), 1)
    unit = jnp.where(row == col, 1.0, 0.0).astype(jnp.bfloat16)

    def fill(geom, vals):
        for t in range(CHUNK // TILE):
            at = t * TILE
            full = jnp.concatenate([geom[:, at : at + TILE], vals[:, at : at + TILE]], axis=0)
            upper = full.astype(jnp.bfloat16)
            lower = (full - upper.astype(jnp.float32)).astype(jnp.bfloat16)
            both = jnp.concatenate([upper, lower], axis=0)
            out_ref[at : at + TILE, :] = lax.dot_general(unit, both, NT, preferred_element_type=jnp.float32)

    @pl.when(pl.program_id(0) < steps)
    def _():
        fill(geom_ref, vals_ref)

    @pl.when(pl.program_id(0) >= steps)
    def _():
        fill(geom_two, vals_two)


def table(geom, vals, geom_two, vals_two):
    cells = geom.shape[1]
    steps = cells // CHUNK
    mine = lambda i: (0, jnp.minimum(i, steps - 1))
    others = lambda i: (0, jnp.maximum(i - steps, 0))
    return pl.pallas_call(
        functools.partial(table_kernel, steps),
        name="table",
        grid=(2 * steps,),
        in_specs=[
            pl.BlockSpec((24, CHUNK), mine),
            pl.BlockSpec((40, CHUNK), mine),
            pl.BlockSpec((24, CHUNK), others),
            pl.BlockSpec((40, CHUNK), others),
        ],
        out_specs=pl.BlockSpec((CHUNK, 2 * FIELDS), lambda i: (i, 0)),
        out_shape=jax.ShapeDtypeStruct((2 * cells, 2 * FIELDS), jnp.float32),
        compiler_params=pltpu.CompilerParams(vmem_limit_bytes=10 << 20),
        cost_estimate=pl.CostEstimate(flops=2 << 30, bytes_accessed=32 << 20, transcendentals=0),
    )(geom, vals, geom_two, vals_two)


GROUP = 8
HEAD = 8


def cross(a, b):
    return (a[1] * b[2] - a[2] * b[1], a[2] * b[0] - a[0] * b[2], a[0] * b[1] - a[1] * b[0])


def dot3(a, b):
    return a[0] * b[0] + a[1] * b[1] + a[2] * b[2]


def newton_values(field, pos):
    geom = [[field(c * 8 + m) for m in range(8)] for c in range(3)]
    x = y = z = None
    for step in range(NEWTON):
        if step == 0:
            misfit = [geom[c][0] - pos[c] for c in range(3)]
            cols = [[geom[c][d + 1] for c in range(3)] for d in range(3)]
        else:
            xy, xz, yz = x * y, x * z, y * z
            misfit, cols = [], [[], [], []]
            for c in range(3):
                g = geom[c]
                dx = g[1] + y * g[4] + z * g[5] + yz * g[7]
                dy = g[2] + x * g[4] + z * g[6] + xz * g[7]
                dz = g[3] + x * g[5] + y * g[6] + xy * g[7]
                misfit.append((g[0] - pos[c]) + x * dx + y * (g[2] + z * g[6]) + z * g[3])
                cols[0].append(dx)
                cols[1].append(dy)
                cols[2].append(dz)
        bc, ca, ab = cross(cols[1], cols[2]), cross(cols[2], cols[0]), cross(cols[0], cols[1])
        determ = dot3(cols[0], bc)
        deltas = [dot3(misfit, side) / determ for side in (bc, ca, ab)]
        if step == 0:
            x, y, z = -deltas[0], -deltas[1], -deltas[2]
        else:
            x, y, z = x - deltas[0], y - deltas[1], z - deltas[2]
    xy, xz, yz = x * y, x * z, y * z
    xyz = xy * z
    results = []
    for k in range(VARS):
        h = [field(24 + k * 8 + m) for m in range(8)]
        results.append(
            (h[0] + x * h[1]) + (y * h[2] + z * h[3]) + (xy * h[4] + xz * h[5]) + (yz * h[6] + xyz * h[7])
        )
    return results


def main_kernel(recv, tab, mono, out, marks, marks_s, order, sets, out_stage, sem):
    devices = recv.shape[0] // (4 * CAP)
    sub = lax.broadcasted_iota(jnp.int32, (8, BLOCK), 0)
    lane = lax.broadcasted_iota(jnp.int32, (8, BLOCK), 1)
    first = jnp.where((sub == 0) & (lane == 0), 1.0, 0.0)
    count = jnp.zeros((8, devices), jnp.float32)
    for s in range(CAP):
        cells = recv[pl.ds(4 * s + 3, devices, stride=4 * CAP), :]
        lead = lax.dot_general(first, cells, NT, preferred_element_type=jnp.float32)
        count = count + jnp.where(lead >= 0.0, 1.0, 0.0)
    before = lax.broadcasted_iota(jnp.int32, (devices, devices), 0)
    after = lax.broadcasted_iota(jnp.int32, (devices, devices), 1)
    lower = jnp.where(before < after, 1.0, 0.0)
    start = jnp.dot(count, lower, preferred_element_type=jnp.float32)
    marks[0:8, :] = start.astype(jnp.int32)
    marks[8:16, :] = count.astype(jnp.int32)
    copy = pltpu.make_async_copy(marks, marks_s, sem.at[2])
    copy.start()
    for j in range(HEAD):
        order[j] = 0
    copy.wait()

    def listing(source, carry):
        at = marks_s[0, source] + HEAD
        for j in range(CAP):
            order[at + j] = source * CAP + j
        return carry

    lax.fori_loop(0, devices, listing, 0, unroll=4)
    total = marks_s[0, devices - 1] + marks_s[8, devices - 1]
    for j in range(3 * GROUP):
        order[HEAD + total + j] = 0
    pairs = (total + 2 * GROUP - 1) // (2 * GROUP)
    masks = [sub == s for s in range(8)]

    def index_copy(p):
        return pltpu.make_async_copy(sets[p]["whole"], sets[p]["index"], sem.at[p])

    def stage(g, p):
        inbox = sets[p]["inbox"]
        for k in range(GROUP):
            e = order[HEAD + g * GROUP + k]
            inbox[pl.ds(k, 4, stride=8), :] = recv[pl.ds(pl.multiple_of(e * 4, 4), 4), :]
        sets[p]["whole"][...] = jnp.maximum(inbox[24:32, :], 0.0).astype(jnp.int32)
        index_copy(p).start()

    def row(i):
        return jnp.broadcast_to(tab[pl.ds(i, 1), :], (8, 2 * FIELDS))

    def gather(p):
        index, rows = sets[p]["index"], sets[p]["rows"]
        sets[p]["pos"][...] = sets[p]["inbox"][0:24, :]
        for q in range(GROUP * BLOCK // 16):
            halves = []
            for h in range(2):
                at = q * 16 + h * 8
                k, u = at // BLOCK, at % BLOCK
                tile = row(index[k, u])
                for s in range(1, 8):
                    tile = jnp.where(masks[s], row(index[k, u + s]), tile)
                halves.append(tile)
            rows[q * 16 : q * 16 + 16, :] = jnp.concatenate(halves, axis=0).astype(jnp.bfloat16)

    def compute(g, p):
        rows, coefs, results = sets[p]["rows"], sets[p]["coefs"], sets[p]["results"]
        for k in range(0, GROUP, 2):
            made = lax.dot_general(
                mono[...], rows[k * BLOCK : (k + 2) * BLOCK, :], NT, preferred_element_type=jnp.float32
            )
            coefs[pl.ds(k, FIELDS, stride=8), :] = made[:, :BLOCK]
            coefs[pl.ds(k + 1, FIELDS, stride=8), :] = made[:, BLOCK:]
        pos = [sets[p]["pos"][c * 8 : c * 8 + 8, :] for c in range(3)]
        made = newton_values(lambda i: coefs[i * 8 : i * 8 + 8, :], pos)
        for v in range(VARS):
            results[v * 8 : v * 8 + 8, :] = made[v]
        for k in range(GROUP):
            e = order[HEAD + g * GROUP + k]
            out[pl.ds(e * VARS, VARS), :] = results[pl.ds(k, VARS, stride=8), :]

    @pl.when(pairs > 0)
    def _():
        stage(0, 0)

    def two(i, carry):
        for p in range(2):
            g = 2 * i + p
            index_copy(p).wait()
            stage(g + 1, 1 - p)
            gather(p)
            compute(g - 1, 1 - p)
        return carry

    lax.fori_loop(0, pairs, two, 0)

    @pl.when(pairs > 0)
    def _():
        index_copy(0).wait()
        compute(2 * pairs - 1, 1)


def main_entry(recv, tab, mono, out, *scratch):
    marks, marks_s, order = scratch[:3]
    names = ("inbox", "whole", "index", "pos", "rows", "coefs", "results")
    sets = [dict(zip(names, scratch[3 + 7 * p : 10 + 7 * p])) for p in range(2)]
    main_kernel(recv, tab, mono, out, marks, marks_s, order, sets, None, scratch[-1])


def main(recv, tab):
    entries = recv.shape[0] // 4
    devices = entries // CAP
    mono = jnp.asarray(monomial_matrix(), jnp.bfloat16)
    one_set = [
        pltpu.VMEM((32, BLOCK), jnp.float32),
        pltpu.VMEM((8, BLOCK), jnp.int32),
        pltpu.SMEM((8, BLOCK), jnp.int32),
        pltpu.VMEM((24, BLOCK), jnp.float32),
        pltpu.VMEM((GROUP * BLOCK, 2 * FIELDS), jnp.bfloat16),
        pltpu.VMEM((8 * FIELDS, BLOCK), jnp.float32),
        pltpu.VMEM((8 * VARS, BLOCK), jnp.float32),
    ]
    return pl.pallas_call(
        main_entry,
        name="main",
        in_specs=[pl.BlockSpec(memory_space=pltpu.VMEM)] * 3,
        out_specs=pl.BlockSpec(memory_space=pltpu.VMEM),
        out_shape=jax.ShapeDtypeStruct((entries * VARS, BLOCK), jnp.float32),
        scratch_shapes=[
            pltpu.VMEM((16, devices), jnp.int32),
            pltpu.SMEM((16, devices), jnp.int32),
            pltpu.SMEM((HEAD + entries + 4 * GROUP,), jnp.int32),
            *one_set,
            *one_set,
            pltpu.SemaphoreType.DMA((3,)),
        ],
        compiler_params=pltpu.CompilerParams(vmem_limit_bytes=28 << 20),
        cost_estimate=pl.CostEstimate(flops=2 << 30, bytes_accessed=20 << 20, transcendentals=0),
    )(recv, tab, mono)


def unpack_kernel(place_ref, answers, out_ref):
    blocks = place_ref.shape[1]

    def one(b, carry):
        at = pl.multiple_of(b * BLOCK, BLOCK)
        out_ref[:, pl.ds(at, BLOCK)] = answers[pl.ds(place_ref[0, b] * VARS, VARS), :]
        return carry

    lax.fori_loop(0, blocks, one, 0, unroll=8)


def unpack(place, answers):
    blocks = place.shape[1]
    return pl.pallas_call(
        unpack_kernel,
        name="unpack",
        in_specs=[pl.BlockSpec(memory_space=pltpu.SMEM), pl.BlockSpec(memory_space=pltpu.VMEM)],
        out_specs=pl.BlockSpec(memory_space=pltpu.VMEM),
        out_shape=jax.ShapeDtypeStruct((VARS, blocks * BLOCK), jnp.float32),
        compiler_params=pltpu.CompilerParams(vmem_limit_bytes=8 << 20),
    )(place, answers)


def per_device(recv_pos, donor_cell, block_owner, cell_geom, cell_values):
    devices = lax.axis_size(AXES)
    blocks = block_owner.shape[0]
    cells_per = cell_geom.shape[1]
    slots = devices * CAP
    swap = [(i, i ^ 1) for i in range(lax.axis_size("brick"))]
    geom_two = lax.ppermute(cell_geom, "brick", swap)
    vals_two = lax.ppermute(cell_values, "brick", swap)
    turn = (lax.axis_index("brick") >> 1 & 1).astype(jnp.int32)[None]
    outgoing, place = pack(
        turn, block_owner.reshape(1, blocks), recv_pos, donor_cell.reshape(blocks, BLOCK), cells_per, slots
    )
    arrived = lax.all_to_all(
        outgoing.reshape(devices, CAP, 4, BLOCK), AXES, split_axis=0, concat_axis=0, tiled=True
    )
    tab = table(cell_geom, cell_values, geom_two, vals_two)
    answer = main(arrived.reshape(slots * 4, BLOCK), tab)
    answers = lax.all_to_all(
        answer.reshape(devices, VARS, CAP, BLOCK), AXES, split_axis=0, concat_axis=0, tiled=True
    )
    return unpack(place, answers.reshape(slots * VARS, BLOCK))


def solution(mesh):
    placed = (
        P(None, AXES),
        P(AXES),
        P(AXES, None),
        P(None, AXES),
        P(None, AXES),
    )
    return jax.shard_map(
        per_device,
        mesh=mesh,
        in_specs=placed,
        out_specs=P(None, AXES),
        check_vma=False,
    )
```

```python
import functools

import jax
import jax.numpy as jnp
import numpy as np
from jax import lax
from jax.experimental import pallas as pl
from jax.experimental.pallas import tpu as pltpu
from jax.sharding import PartitionSpec as P

BLOCK = 128
CAP = 4
NEWTON = 3
VARS = 5
FIELDS = 64
AXES = ("near", "brick")
NT = (((1,), (1,)), ((), ()))


def monomial_matrix():
    signs = np.array([[2 * (v >> d & 1) - 1 for v in range(8)] for d in range(3)])
    rows = [np.ones(8), signs[0], signs[1], signs[2]]
    rows += [signs[0] * signs[1], signs[0] * signs[2], signs[1] * signs[2]]
    rows += [signs[0] * signs[1] * signs[2]]
    block = np.stack(rows) / 8.0
    full = np.kron(np.eye(FIELDS // 8), block)
    return np.concatenate([full, full], axis=1).astype(np.float32)


def pack_kernel(cells_per, turn_ref, owner_hbm, pos_hbm, cell_hbm, out_hbm, place_ref, owner_ref, pos_ref, cell_ref, out_ref, spot, lists, sem):
    blocks = owner_ref.shape[1]
    fetches = [
        pltpu.make_async_copy(source, target, sem.at[i])
        for i, (source, target) in enumerate(((owner_hbm, owner_ref), (pos_hbm, pos_ref), (cell_hbm, cell_ref)))
    ]
    for fetch in fetches:
        fetch.start()
    out_ref[...] = jnp.full(out_ref.shape, -1.0, jnp.float32)
    fetches[0].wait()
    owner = owner_ref[...]
    key = jnp.broadcast_to((owner >> 1).astype(jnp.float32), (blocks, blocks))
    earlier = lax.broadcasted_iota(jnp.int32, (blocks, blocks), 0)
    later = lax.broadcasted_iota(jnp.int32, (blocks, blocks), 1)
    same = jnp.where((key.T == key) & (earlier < later), 1.0, 0.0)
    rank = jnp.sum(same, axis=0, keepdims=True).astype(jnp.int32)
    core = (rank + turn_ref[0]) & 1
    place = ((owner & -2) + core) * CAP + (rank >> 1)
    place_ref[...] = place
    spot[0:1, :] = place
    spot[1:2, :] = ((owner ^ core) & 1) * cells_per
    copy = pltpu.make_async_copy(spot, lists, sem.at[3])
    copy.start()
    copy.wait()
    fetches[1].wait()
    fetches[2].wait()

    def one(b, carry):
        at = pl.multiple_of(b * BLOCK, BLOCK)
        e = lists[0, b]
        out_ref[e, 0:3, :] = pos_ref[:, pl.ds(at, BLOCK)]
        out_ref[e, 3:4, :] = (cell_ref[pl.ds(b, 1), :] + lists[1, b]).astype(jnp.float32)
        return carry

    lax.fori_loop(0, blocks, one, 0, unroll=8)
    done = pltpu.make_async_copy(out_ref, out_hbm, sem.at[0])
    done.start()
    done.wait()


def pack(turn, owner, pos, cell, cells_per, slots):
    blocks = owner.shape[1]
    return pl.pallas_call(
        functools.partial(pack_kernel, cells_per),
        name="pack",
        in_specs=[pl.BlockSpec(memory_space=pltpu.SMEM)] + [pl.BlockSpec(memory_space=pl.ANY)] * 3,
        out_specs=[pl.BlockSpec(memory_space=pl.ANY), pl.BlockSpec(memory_space=pltpu.VMEM)],
        out_shape=[
            jax.ShapeDtypeStruct((slots, 4, BLOCK), jnp.float32),
            jax.ShapeDtypeStruct((1, blocks), jnp.int32),
        ],
        scratch_shapes=[
            pltpu.VMEM(owner.shape, jnp.int32),
            pltpu.VMEM(pos.shape, jnp.float32),
            pltpu.VMEM(cell.shape, jnp.int32),
            pltpu.VMEM((slots, 4, BLOCK), jnp.float32),
            pltpu.VMEM((2, blocks), jnp.int32),
            pltpu.SMEM((2, blocks), jnp.int32),
            pltpu.SemaphoreType.DMA((4,)),
        ],
        compiler_params=pltpu.CompilerParams(vmem_limit_bytes=56 << 20),
    )(turn, owner, pos, cell)


CHUNK = 2048


def table_kernel(geom_ref, vals_ref, geom_two, vals_two, out_ref):
    for at in range(0, CHUNK, BLOCK):
        parts = [ref[:, at : at + BLOCK] for ref in (geom_ref, vals_ref, geom_two, vals_two)]
        out_ref[at : at + BLOCK, :] = jnp.concatenate(parts, axis=0).T


def table(geom, vals, geom_two, vals_two):
    cells = geom.shape[1]
    spot = lambda i: (0, i)
    return pl.pallas_call(
        table_kernel,
        name="table",
        grid=(cells // CHUNK,),
        in_specs=[
            pl.BlockSpec((24, CHUNK), spot),
            pl.BlockSpec((40, CHUNK), spot),
            pl.BlockSpec((24, CHUNK), spot),
            pl.BlockSpec((40, CHUNK), spot),
        ],
        out_specs=pl.BlockSpec((CHUNK, 2 * FIELDS), lambda i: (i, 0)),
        out_shape=jax.ShapeDtypeStruct((cells, 2 * FIELDS), jnp.float32),
        compiler_params=pltpu.CompilerParams(vmem_limit_bytes=16 << 20),
        cost_estimate=pl.CostEstimate(flops=2 << 30, bytes_accessed=32 << 20, transcendentals=0),
    )(geom, vals, geom_two, vals_two)


GROUP = 8
HEAD = 8


def cross(a, b):
    return (a[1] * b[2] - a[2] * b[1], a[2] * b[0] - a[0] * b[2], a[0] * b[1] - a[1] * b[0])


def dot3(a, b):
    return a[0] * b[0] + a[1] * b[1] + a[2] * b[2]


def newton_values(field, pos):
    geom = [[field(c * 8 + m) for m in range(8)] for c in range(3)]
    x = y = z = None
    for step in range(NEWTON):
        if step == 0:
            misfit = [geom[c][0] - pos[c] for c in range(3)]
            cols = [[geom[c][d + 1] for c in range(3)] for d in range(3)]
        else:
            xy, xz, yz = x * y, x * z, y * z
            misfit, cols = [], [[], [], []]
            for c in range(3):
                g = geom[c]
                dx = g[1] + y * g[4] + z * g[5] + yz * g[7]
                dy = g[2] + x * g[4] + z * g[6] + xz * g[7]
                dz = g[3] + x * g[5] + y * g[6] + xy * g[7]
                misfit.append((g[0] - pos[c]) + x * dx + y * (g[2] + z * g[6]) + z * g[3])
                cols[0].append(dx)
                cols[1].append(dy)
                cols[2].append(dz)
        bc, ca, ab = cross(cols[1], cols[2]), cross(cols[2], cols[0]), cross(cols[0], cols[1])
        determ = dot3(cols[0], bc)
        deltas = [dot3(misfit, side) / determ for side in (bc, ca, ab)]
        if step == 0:
            x, y, z = -deltas[0], -deltas[1], -deltas[2]
        else:
            x, y, z = x - deltas[0], y - deltas[1], z - deltas[2]
    xy, xz, yz = x * y, x * z, y * z
    xyz = xy * z
    results = []
    for k in range(VARS):
        h = [field(24 + k * 8 + m) for m in range(8)]
        results.append(
            (h[0] + x * h[1]) + (y * h[2] + z * h[3]) + (xy * h[4] + xz * h[5]) + (yz * h[6] + xyz * h[7])
        )
    return results


def main_kernel(recv, tab_hbm, mono, out, tab, marks, marks_s, order, sets, sem):
    devices = recv.shape[0] // (4 * CAP)
    cells_per = tab.shape[0]
    fetch = pltpu.make_async_copy(tab_hbm, tab, sem.at[3])
    fetch.start()
    sub = lax.broadcasted_iota(jnp.int32, (8, BLOCK), 0)
    lane = lax.broadcasted_iota(jnp.int32, (8, BLOCK), 1)
    first = jnp.where((sub == 0) & (lane == 0), 1.0, 0.0)
    count = jnp.zeros((8, devices), jnp.float32)
    for s in range(CAP):
        cells = recv[pl.ds(4 * s + 3, devices, stride=4 * CAP), :]
        lead = lax.dot_general(first, cells, NT, preferred_element_type=jnp.float32)
        count = count + jnp.where(lead >= 0.0, 1.0, 0.0)
    before = lax.broadcasted_iota(jnp.int32, (devices, devices), 0)
    after = lax.broadcasted_iota(jnp.int32, (devices, devices), 1)
    lower = jnp.where(before < after, 1.0, 0.0)
    start = jnp.dot(count, lower, preferred_element_type=jnp.float32)
    marks[0:8, :] = start.astype(jnp.int32)
    marks[8:16, :] = count.astype(jnp.int32)
    copy = pltpu.make_async_copy(marks, marks_s, sem.at[2])
    copy.start()
    for j in range(HEAD):
        order[j] = 0
    copy.wait()

    def listing(source, carry):
        at = marks_s[0, source] + HEAD
        for j in range(CAP):
            order[at + j] = source * CAP + j
        return carry

    lax.fori_loop(0, devices, listing, 0, unroll=4)
    total = marks_s[0, devices - 1] + marks_s[8, devices - 1]
    for j in range(4 * GROUP):
        order[HEAD + total + j] = 0
    pairs = (total + 2 * GROUP - 1) // (2 * GROUP)
    masks = [sub == s for s in range(8)]

    def index_copy(p):
        return pltpu.make_async_copy(sets[p]["whole"], sets[p]["index"], sem.at[p])

    def stage(g, p):
        inbox = sets[p]["inbox"]
        for k in range(GROUP):
            e = order[HEAD + g * GROUP + k]
            inbox[pl.ds(k, 4, stride=8), :] = recv[pl.ds(pl.multiple_of(e * 4, 4), 4), :]
        cell = jnp.maximum(inbox[24:32, :], 0.0).astype(jnp.int32)
        sets[p]["whole"][...] = jnp.where(cell >= cells_per, cell - cells_per, cell)

    def row(i):
        return jnp.broadcast_to(tab[pl.ds(i, 1), :], (8, 2 * FIELDS))

    def gather(p):
        index, inbox = sets[p]["index"], sets[p]["inbox"]
        sets[p]["pos"][...] = inbox[0:24, :]
        for k in range(GROUP):
            theirs = jnp.broadcast_to(inbox[24 + k : 25 + k, :], (8, BLOCK)) >= float(cells_per)
            keep = theirs == (lane >= FIELDS)
            for u in range(0, BLOCK, 16):
                tiles = []
                for h in (u, u + 8):
                    tile = row(index[k, h])
                    for s in range(1, 8):
                        tile = jnp.where(masks[s], row(index[k, h + s]), tile)
                    tiles.append(jnp.where(keep, tile, 0.0))
                full = jnp.concatenate(tiles, axis=0)
                upper = full.astype(jnp.bfloat16)
                at = k * BLOCK + u
                sets[p]["upper"][at : at + 16, :] = upper
                sets[p]["lower"][at : at + 16, :] = (full - upper.astype(jnp.float32)).astype(jnp.bfloat16)

    def compute(g, p):
        coefs, results = sets[p]["coefs"], sets[p]["results"]
        for k in range(0, GROUP, 2):
            made = sum(
                lax.dot_general(
                    mono[...],
                    sets[p][part][k * BLOCK : (k + 2) * BLOCK, :],
                    NT,
                    preferred_element_type=jnp.float32,
                )
                for part in ("lower", "upper")
            )
            coefs[pl.ds(k, FIELDS, stride=8), :] = made[:, :BLOCK]
            coefs[pl.ds(k + 1, FIELDS, stride=8), :] = made[:, BLOCK:]
        pos = [sets[p]["pos"][c * 8 : c * 8 + 8, :] for c in range(3)]
        made = newton_values(lambda i: coefs[i * 8 : i * 8 + 8, :], pos)
        for v in range(VARS):
            results[v * 8 : v * 8 + 8, :] = made[v]
        for k in range(GROUP):
            e = order[HEAD + g * GROUP + k]
            out[pl.ds(e * VARS, VARS), :] = results[pl.ds(k, VARS, stride=8), :]

    stage(0, 0)
    index_copy(0).start()
    stage(1, 1)
    fetch.wait()

    def two(i, carry):
        for p in range(2):
            g = 2 * i + p
            index_copy(1 - p).start()
            index_copy(p).wait()
            gather(p)
            compute(g - 1, 1 - p)
            stage(g + 2, p)
        return carry

    lax.fori_loop(0, pairs, two, 0)

    index_copy(0).wait()

    @pl.when(pairs > 0)
    def _():
        compute(2 * pairs - 1, 1)


def main_entry(recv, tab, mono, out, *scratch):
    names = ("inbox", "whole", "index", "pos", "upper", "lower", "coefs", "results")
    sets = [dict(zip(names, scratch[4 + 8 * p : 12 + 8 * p])) for p in range(2)]
    main_kernel(recv, tab, mono, out, *scratch[:4], sets, scratch[-1])


def main(recv, tab):
    entries = recv.shape[0] // 4
    devices = entries // CAP
    mono = jnp.asarray(monomial_matrix(), jnp.bfloat16)
    one_set = [
        pltpu.VMEM((32, BLOCK), jnp.float32),
        pltpu.VMEM((8, BLOCK), jnp.int32),
        pltpu.SMEM((8, BLOCK), jnp.int32),
        pltpu.VMEM((24, BLOCK), jnp.float32),
        pltpu.VMEM((GROUP * BLOCK, 2 * FIELDS), jnp.bfloat16),
        pltpu.VMEM((GROUP * BLOCK, 2 * FIELDS), jnp.bfloat16),
        pltpu.VMEM((8 * FIELDS, BLOCK), jnp.float32),
        pltpu.VMEM((8 * VARS, BLOCK), jnp.float32),
    ]
    return pl.pallas_call(
        main_entry,
        name="main",
        in_specs=[
            pl.BlockSpec(memory_space=pltpu.VMEM),
            pl.BlockSpec(memory_space=pl.ANY),
            pl.BlockSpec(memory_space=pltpu.VMEM),
        ],
        out_specs=pl.BlockSpec(memory_space=pltpu.VMEM),
        out_shape=jax.ShapeDtypeStruct((entries * VARS, BLOCK), jnp.float32),
        scratch_shapes=[
            pltpu.VMEM(tab.shape, jnp.float32),
            pltpu.VMEM((16, devices), jnp.int32),
            pltpu.SMEM((16, devices), jnp.int32),
            pltpu.SMEM((HEAD + entries + 4 * GROUP,), jnp.int32),
            *one_set,
            *one_set,
            pltpu.SemaphoreType.DMA((4,)),
        ],
        compiler_params=pltpu.CompilerParams(vmem_limit_bytes=28 << 20),
        cost_estimate=pl.CostEstimate(flops=2 << 30, bytes_accessed=20 << 20, transcendentals=0),
    )(recv, tab, mono)


def unpack_kernel(place_ref, answers, out_ref):
    blocks = place_ref.shape[1]

    def one(b, carry):
        at = pl.multiple_of(b * BLOCK, BLOCK)
        out_ref[:, pl.ds(at, BLOCK)] = answers[pl.ds(place_ref[0, b] * VARS, VARS), :]
        return carry

    lax.fori_loop(0, blocks, one, 0, unroll=8)


def unpack(place, answers):
    blocks = place.shape[1]
    return pl.pallas_call(
        unpack_kernel,
        name="unpack",
        in_specs=[pl.BlockSpec(memory_space=pltpu.SMEM), pl.BlockSpec(memory_space=pltpu.VMEM)],
        out_specs=pl.BlockSpec(memory_space=pltpu.VMEM),
        out_shape=jax.ShapeDtypeStruct((VARS, blocks * BLOCK), jnp.float32),
        compiler_params=pltpu.CompilerParams(vmem_limit_bytes=8 << 20),
    )(place, answers)


def per_device(recv_pos, donor_cell, block_owner, cell_geom, cell_values):
    devices = lax.axis_size(AXES)
    blocks = block_owner.shape[0]
    cells_per = cell_geom.shape[1]
    slots = devices * CAP
    swap = [(i, i ^ 1) for i in range(lax.axis_size("brick"))]
    geom_two = lax.ppermute(cell_geom, "brick", swap)
    vals_two = lax.ppermute(cell_values, "brick", swap)
    turn = (lax.axis_index("brick") >> 1 & 1).astype(jnp.int32)[None]
    outgoing, place = pack(
        turn, block_owner.reshape(1, blocks), recv_pos, donor_cell.reshape(blocks, BLOCK), cells_per, slots
    )
    arrived = lax.all_to_all(
        outgoing.reshape(devices, CAP, 4, BLOCK), AXES, split_axis=0, concat_axis=0, tiled=True
    )
    tab = table(cell_geom, cell_values, geom_two, vals_two)
    answer = main(arrived.reshape(slots * 4, BLOCK), tab)
    answers = lax.all_to_all(
        answer.reshape(devices, VARS, CAP, BLOCK), AXES, split_axis=0, concat_axis=0, tiled=True
    )
    return unpack(place, answers.reshape(slots * VARS, BLOCK))


def solution(mesh):
    placed = (
        P(None, AXES),
        P(AXES),
        P(AXES, None),
        P(None, AXES),
        P(None, AXES),
    )
    return jax.shard_map(
        per_device,
        mesh=mesh,
        in_specs=placed,
        out_specs=P(None, AXES),
        check_vma=False,
    )
```

```python
import functools

import jax
import jax.numpy as jnp
import numpy as np
from jax import lax
from jax.experimental import pallas as pl
from jax.experimental.pallas import tpu as pltpu
from jax.sharding import PartitionSpec as P

BLOCK = 128
CAP = 4
NEWTON = 3
VARS = 5
FIELDS = 64
AXES = ("near", "brick")
NT = (((1,), (1,)), ((), ()))


def monomial_matrix():
    signs = np.array([[2 * (v >> d & 1) - 1 for v in range(8)] for d in range(3)])
    rows = [np.ones(8), signs[0], signs[1], signs[2]]
    rows += [signs[0] * signs[1], signs[0] * signs[2], signs[1] * signs[2]]
    rows += [signs[0] * signs[1] * signs[2]]
    block = np.stack(rows) / 8.0
    full = np.kron(np.eye(FIELDS // 8), block)
    return np.concatenate([full] * 4, axis=1).astype(np.float32)


def pack_kernel(cells_per, turn_ref, owner_hbm, pos_hbm, cell_hbm, out_hbm, place_ref, owner_ref, pos_ref, cell_ref, out_ref, spot, lists, sem):
    blocks = owner_ref.shape[1]
    fetches = [
        pltpu.make_async_copy(source, target, sem.at[i])
        for i, (source, target) in enumerate(((owner_hbm, owner_ref), (pos_hbm, pos_ref), (cell_hbm, cell_ref)))
    ]
    for fetch in fetches:
        fetch.start()
    out_ref[...] = jnp.full(out_ref.shape, -1.0, jnp.float32)
    fetches[0].wait()
    owner = owner_ref[...]
    key = jnp.broadcast_to((owner >> 1).astype(jnp.float32), (blocks, blocks))
    earlier = lax.broadcasted_iota(jnp.int32, (blocks, blocks), 0)
    later = lax.broadcasted_iota(jnp.int32, (blocks, blocks), 1)
    same = jnp.where((key.T == key) & (earlier < later), 1.0, 0.0)
    rank = jnp.sum(same, axis=0, keepdims=True).astype(jnp.int32)
    core = (rank + turn_ref[0]) & 1
    place = ((owner & -2) + core) * CAP + (rank >> 1)
    place_ref[...] = place * VARS
    spot[0:1, :] = place
    spot[1:2, :] = ((owner ^ core) & 1) * cells_per
    copy = pltpu.make_async_copy(spot, lists, sem.at[3])
    copy.start()
    copy.wait()
    fetches[1].wait()
    fetches[2].wait()

    for b in range(blocks):
        e = lists[0, b]
        out_ref[e, 0:3, :] = pos_ref[:, b * BLOCK : (b + 1) * BLOCK]
        out_ref[e, 3:4, :] = (cell_ref[b : b + 1, :] + lists[1, b]).astype(jnp.float32)
    done = pltpu.make_async_copy(out_ref, out_hbm, sem.at[0])
    done.start()
    done.wait()


def pack(turn, owner, pos, cell, cells_per, slots):
    blocks = owner.shape[1]
    return pl.pallas_call(
        functools.partial(pack_kernel, cells_per),
        name="pack",
        in_specs=[pl.BlockSpec(memory_space=pltpu.SMEM)] + [pl.BlockSpec(memory_space=pl.ANY)] * 3,
        out_specs=[pl.BlockSpec(memory_space=pl.ANY), pl.BlockSpec(memory_space=pltpu.VMEM)],
        out_shape=[
            jax.ShapeDtypeStruct((slots, 4, BLOCK), jnp.float32),
            jax.ShapeDtypeStruct((1, blocks), jnp.int32),
        ],
        scratch_shapes=[
            pltpu.VMEM(owner.shape, jnp.int32),
            pltpu.VMEM(pos.shape, jnp.float32),
            pltpu.VMEM(cell.shape, jnp.int32),
            pltpu.VMEM((slots, 4, BLOCK), jnp.float32),
            pltpu.VMEM((2, blocks), jnp.int32),
            pltpu.SMEM((2, blocks), jnp.int32),
            pltpu.SemaphoreType.DMA((4,)),
        ],
        compiler_params=pltpu.CompilerParams(vmem_limit_bytes=56 << 20),
    )(turn, owner, pos, cell)


CHUNK = 2048


def table_kernel(geom_ref, vals_ref, geom_two, vals_two, out_ref):
    for at in range(0, CHUNK, BLOCK):
        parts = [ref[:, at : at + BLOCK] for ref in (geom_ref, vals_ref, geom_two, vals_two)]
        out_ref[at : at + BLOCK, :] = jnp.concatenate(parts, axis=0).T


def table(geom, vals, geom_two, vals_two):
    cells = geom.shape[1]
    spot = lambda i: (0, i)
    return pl.pallas_call(
        table_kernel,
        name="table",
        grid=(cells // CHUNK,),
        in_specs=[
            pl.BlockSpec((24, CHUNK), spot),
            pl.BlockSpec((40, CHUNK), spot),
            pl.BlockSpec((24, CHUNK), spot),
            pl.BlockSpec((40, CHUNK), spot),
        ],
        out_specs=pl.BlockSpec((CHUNK, 2 * FIELDS), lambda i: (i, 0)),
        out_shape=jax.ShapeDtypeStruct((cells, 2 * FIELDS), jnp.float32),
        compiler_params=pltpu.CompilerParams(vmem_limit_bytes=16 << 20),
        cost_estimate=pl.CostEstimate(flops=2 << 30, bytes_accessed=32 << 20, transcendentals=0),
    )(geom, vals, geom_two, vals_two)


GROUP = 8
HEAD = 8
READY = 6
AHEAD = 4


def cross(a, b):
    return (a[1] * b[2] - a[2] * b[1], a[2] * b[0] - a[0] * b[2], a[0] * b[1] - a[1] * b[0])


def dot3(a, b):
    return a[0] * b[0] + a[1] * b[1] + a[2] * b[2]


def newton_values(field, pos):
    geom = [[field(c * 8 + m) for m in range(8)] for c in range(3)]
    x = y = z = None
    for step in range(NEWTON):
        if step == 0:
            misfit = [geom[c][0] - pos[c] for c in range(3)]
            cols = [[geom[c][d + 1] for c in range(3)] for d in range(3)]
        else:
            xy, xz, yz = x * y, x * z, y * z
            misfit, cols = [], [[], [], []]
            for c in range(3):
                g = geom[c]
                dx = g[1] + y * g[4] + z * g[5] + yz * g[7]
                dy = g[2] + x * g[4] + z * g[6] + xz * g[7]
                dz = g[3] + x * g[5] + y * g[6] + xy * g[7]
                misfit.append((g[0] - pos[c]) + x * dx + y * (g[2] + z * g[6]) + z * g[3])
                cols[0].append(dx)
                cols[1].append(dy)
                cols[2].append(dz)
        bc, ca, ab = cross(cols[1], cols[2]), cross(cols[2], cols[0]), cross(cols[0], cols[1])
        determ = dot3(cols[0], bc)
        deltas = [dot3(misfit, side) / determ for side in (bc, ca, ab)]
        if step == 0:
            x, y, z = -deltas[0], -deltas[1], -deltas[2]
        else:
            x, y, z = x - deltas[0], y - deltas[1], z - deltas[2]
    xy, xz, yz = x * y, x * z, y * z
    xyz = xy * z
    results = []
    for k in range(VARS):
        h = [field(24 + k * 8 + m) for m in range(8)]
        results.append(
            (h[0] + x * h[1]) + (y * h[2] + z * h[3]) + (xy * h[4] + xz * h[5]) + (yz * h[6] + xyz * h[7])
        )
    return results


def main_kernel(recv, tab_hbm, mono, out, tab, marks, marks_s, order, sets, sem):
    devices = recv.shape[0] // (4 * CAP)
    cells_per = tab.shape[0]
    fetch = pltpu.make_async_copy(tab_hbm, tab, sem.at[3])
    fetch.start()
    sub = lax.broadcasted_iota(jnp.int32, (8, BLOCK), 0)
    lane = lax.broadcasted_iota(jnp.int32, (8, BLOCK), 1)
    first = jnp.where((sub == 0) & (lane == 0), 1.0, 0.0)
    count = jnp.zeros((8, devices), jnp.float32)
    for s in range(CAP):
        cells = recv[pl.ds(4 * s + 3, devices, stride=4 * CAP), :]
        lead = lax.dot_general(first, cells, NT, preferred_element_type=jnp.float32)
        count = count + jnp.where(lead >= 0.0, 1.0, 0.0)
    before = lax.broadcasted_iota(jnp.int32, (devices, devices), 0)
    after = lax.broadcasted_iota(jnp.int32, (devices, devices), 1)
    lower = jnp.where(before < after, 1.0, 0.0)
    start = jnp.dot(count, lower, preferred_element_type=jnp.float32)
    marks[0:8, :] = start.astype(jnp.int32)
    marks[8:16, :] = count.astype(jnp.int32)
    copy = pltpu.make_async_copy(marks, marks_s, sem.at[2])
    copy.start()
    for j in range(HEAD):
        order[j] = 0
    copy.wait()

    def listing(source, carry):
        at = marks_s[0, source] + HEAD
        for j in range(CAP):
            order[at + j] = source * CAP + j
        return carry

    lax.fori_loop(0, devices, listing, 0, unroll=4)
    total = marks_s[0, devices - 1] + marks_s[8, devices - 1]
    for j in range(4 * GROUP):
        order[HEAD + total + j] = 0
    pairs = (total + 2 * GROUP - 1) // (2 * GROUP)
    masks = [sub == s for s in range(8)]

    def index_copy(p):
        return pltpu.make_async_copy(sets[p]["whole"], sets[p]["index"], sem.at[p])

    def stage(g, p):
        inbox = sets[p]["inbox"]
        for k in range(GROUP):
            e = order[HEAD + g * GROUP + k]
            inbox[pl.ds(k, 4, stride=8), :] = recv[pl.ds(pl.multiple_of(e * 4, 4), 4), :]
        cell = jnp.maximum(inbox[24:32, :], 0.0).astype(jnp.int32)
        sets[p]["whole"][...] = jnp.where(cell >= cells_per, cell - cells_per, cell)

    def row(i):
        return jnp.broadcast_to(tab[pl.ds(i, 1), :], (8, 2 * FIELDS))

    def look(p, k, ready):
        index, inbox = sets[p]["index"], sets[p]["inbox"]
        theirs = jnp.broadcast_to(inbox[24 + k : 25 + k, :], (8, BLOCK)) >= float(cells_per)
        keep = (theirs == (lane >= FIELDS)) & ready
        for u in range(0, BLOCK, 16):
            tiles = []
            for h in (u, u + 8):
                tile = row(index[k, h])
                for s in range(1, 8):
                    tile = jnp.where(masks[s], row(index[k, h + s]), tile)
                tiles.append(jnp.where(keep, tile, 0.0))
            full = jnp.concatenate(tiles, axis=0)
            upper = full.astype(jnp.bfloat16)
            at = k * BLOCK + u
            sets[p]["rows"][at : at + 16, : 2 * FIELDS] = upper
            sets[p]["rows"][at : at + 16, 2 * FIELDS :] = (full - upper.astype(jnp.float32)).astype(jnp.bfloat16)

    def product(p, k):
        made = lax.dot_general(
            mono[...], sets[p]["rows"][k * BLOCK : (k + 2) * BLOCK, :], NT, preferred_element_type=jnp.float32
        )
        sets[p]["coefs"][pl.ds(k, FIELDS, stride=8), :] = made[:, :BLOCK]
        sets[p]["coefs"][pl.ds(k + 1, FIELDS, stride=8), :] = made[:, BLOCK:]

    def solve(g, p):
        for k in range(AHEAD, GROUP, 2):
            product(p, k)
        coefs, results = sets[p]["coefs"], sets[p]["results"]
        pos = [sets[p]["pos"][c * 8 : c * 8 + 8, :] for c in range(3)]
        made = newton_values(lambda i: coefs[i * 8 : i * 8 + 8, :], pos)
        for v in range(VARS):
            results[v * 8 : v * 8 + 8, :] = made[v]
        for k in range(GROUP):
            e = order[HEAD + g * GROUP + k]
            out[pl.ds(e * VARS, VARS), :] = results[pl.ds(k, VARS, stride=8), :]
        return (made[4] <= 0.0) | (made[4] > 0.0) | (made[4] != made[4])

    stage(0, 0)
    index_copy(0).start()
    stage(1, 1)
    fetch.wait()

    def two(i, carry):
        for p in range(2):
            g = 2 * i + p
            index_copy(1 - p).start()
            index_copy(p).wait()
            sets[p]["pos"][...] = sets[p]["inbox"][0:24, :]
            ready = solve(g - 1, 1 - p)
            for k in range(GROUP):
                look(p, k, ready if k >= READY else True)
                if k % 2 and k < AHEAD:
                    product(p, k - 1)
            stage(g + 2, p)
        return carry

    lax.fori_loop(0, pairs, two, 0)

    index_copy(0).wait()

    @pl.when(pairs > 0)
    def _():
        solve(2 * pairs - 1, 1)


def main_entry(recv, tab, mono, out, *scratch):
    names = ("inbox", "whole", "index", "pos", "rows", "coefs", "results")
    sets = [dict(zip(names, scratch[4 + 7 * p : 11 + 7 * p])) for p in range(2)]
    main_kernel(recv, tab, mono, out, *scratch[:4], sets, scratch[-1])


def main(recv, tab):
    entries = recv.shape[0] // 4
    devices = entries // CAP
    mono = jnp.asarray(monomial_matrix(), jnp.bfloat16)
    one_set = [
        pltpu.VMEM((32, BLOCK), jnp.float32),
        pltpu.VMEM((8, BLOCK), jnp.int32),
        pltpu.SMEM((8, BLOCK), jnp.int32),
        pltpu.VMEM((24, BLOCK), jnp.float32),
        pltpu.VMEM((GROUP * BLOCK, 4 * FIELDS), jnp.bfloat16),
        pltpu.VMEM((8 * FIELDS, BLOCK), jnp.float32),
        pltpu.VMEM((8 * VARS, BLOCK), jnp.float32),
    ]
    return pl.pallas_call(
        main_entry,
        name="main",
        in_specs=[
            pl.BlockSpec(memory_space=pltpu.VMEM),
            pl.BlockSpec(memory_space=pl.ANY),
            pl.BlockSpec(memory_space=pltpu.VMEM),
        ],
        out_specs=pl.BlockSpec(memory_space=pltpu.VMEM),
        out_shape=jax.ShapeDtypeStruct((entries * VARS, BLOCK), jnp.float32),
        scratch_shapes=[
            pltpu.VMEM(tab.shape, jnp.float32),
            pltpu.VMEM((16, devices), jnp.int32),
            pltpu.SMEM((16, devices), jnp.int32),
            pltpu.SMEM((HEAD + entries + 4 * GROUP,), jnp.int32),
            *one_set,
            *one_set,
            pltpu.SemaphoreType.DMA((4,)),
        ],
        compiler_params=pltpu.CompilerParams(vmem_limit_bytes=54 << 20),
        cost_estimate=pl.CostEstimate(flops=2 << 30, bytes_accessed=20 << 20, transcendentals=0),
    )(recv, tab, mono)


def unpack_kernel(place_ref, answers, out_ref):
    blocks = place_ref.shape[1]

    for b in range(blocks):
        out_ref[:, b * BLOCK : (b + 1) * BLOCK] = answers[pl.ds(place_ref[0, b], VARS), :]


def unpack(place, answers):
    blocks = place.shape[1]
    return pl.pallas_call(
        unpack_kernel,
        name="unpack",
        in_specs=[pl.BlockSpec(memory_space=pltpu.SMEM), pl.BlockSpec(memory_space=pltpu.VMEM)],
        out_specs=pl.BlockSpec(memory_space=pltpu.VMEM),
        out_shape=jax.ShapeDtypeStruct((VARS, blocks * BLOCK), jnp.float32),
        compiler_params=pltpu.CompilerParams(vmem_limit_bytes=8 << 20),
    )(place, answers)


def per_device(recv_pos, donor_cell, block_owner, cell_geom, cell_values):
    devices = lax.axis_size(AXES)
    blocks = block_owner.shape[0]
    cells_per = cell_geom.shape[1]
    slots = devices * CAP
    swap = [(i, i ^ 1) for i in range(lax.axis_size("brick"))]
    geom_two = lax.ppermute(cell_geom, "brick", swap)
    vals_two = lax.ppermute(cell_values, "brick", swap)
    turn = (lax.axis_index("brick") >> 1 & 1).astype(jnp.int32)[None]
    outgoing, place = pack(
        turn, block_owner.reshape(1, blocks), recv_pos, donor_cell.reshape(blocks, BLOCK), cells_per, slots
    )
    arrived = lax.all_to_all(
        outgoing.reshape(devices, CAP, 4, BLOCK), AXES, split_axis=0, concat_axis=0, tiled=True
    )
    tab = table(cell_geom, cell_values, geom_two, vals_two)
    answer = main(arrived.reshape(slots * 4, BLOCK), tab)
    answers = lax.all_to_all(
        answer.reshape(devices, VARS, CAP, BLOCK), AXES, split_axis=0, concat_axis=0, tiled=True
    )
    return unpack(place, answers.reshape(slots * VARS, BLOCK))


def solution(mesh):
    placed = (
        P(None, AXES),
        P(AXES),
        P(AXES, None),
        P(None, AXES),
        P(None, AXES),
    )
    return jax.shard_map(
        per_device,
        mesh=mesh,
        in_specs=placed,
        out_specs=P(None, AXES),
        check_vma=False,
    )
```

```python
import functools

import jax
import jax.numpy as jnp
import numpy as np
from jax import lax
from jax.experimental import pallas as pl
from jax.experimental.pallas import tpu as pltpu
from jax.sharding import PartitionSpec as P

BLOCK = 128
CAP = 4
NEWTON = 3
VARS = 5
FIELDS = 64
AXES = ("near", "brick")
NT = (((1,), (1,)), ((), ()))


def monomial_matrix():
    signs = np.array([[2 * (v >> d & 1) - 1 for v in range(8)] for d in range(3)])
    rows = [np.ones(8), signs[0], signs[1], signs[2]]
    rows += [signs[0] * signs[1], signs[0] * signs[2], signs[1] * signs[2]]
    rows += [signs[0] * signs[1] * signs[2]]
    block = np.stack(rows) / 8.0
    full = np.kron(np.eye(FIELDS // 8), block)
    return np.concatenate([full] * 4, axis=1).astype(np.float32)


def pack_kernel(cells_per, turn_ref, owner_hbm, pos_hbm, cell_hbm, out_hbm, place_ref, owner_ref, pos_ref, cell_ref, out_ref, spot, lists, sem):
    blocks = owner_ref.shape[1]
    fetches = [
        pltpu.make_async_copy(source, target, sem.at[i])
        for i, (source, target) in enumerate(((owner_hbm, owner_ref), (pos_hbm, pos_ref), (cell_hbm, cell_ref)))
    ]
    for fetch in fetches:
        fetch.start()
    out_ref[...] = jnp.full(out_ref.shape, -1.0, jnp.float32)
    fetches[0].wait()
    owner = owner_ref[...]
    key = jnp.broadcast_to((owner >> 1).astype(jnp.float32), (blocks, blocks))
    earlier = lax.broadcasted_iota(jnp.int32, (blocks, blocks), 0)
    later = lax.broadcasted_iota(jnp.int32, (blocks, blocks), 1)
    same = jnp.where((key.T == key) & (earlier < later), 1.0, 0.0)
    rank = jnp.sum(same, axis=0, keepdims=True).astype(jnp.int32)
    core = (rank + turn_ref[0]) & 1
    place = ((owner & -2) + core) * CAP + (rank >> 1)
    place_ref[...] = place * VARS
    spot[0:1, :] = place
    spot[1:2, :] = ((owner ^ core) & 1) * cells_per
    copy = pltpu.make_async_copy(spot, lists, sem.at[3])
    copy.start()
    copy.wait()
    fetches[1].wait()
    fetches[2].wait()

    for b in range(blocks):
        e = lists[0, b]
        out_ref[e, 0:3, :] = pos_ref[:, b * BLOCK : (b + 1) * BLOCK]
        out_ref[e, 3:4, :] = (cell_ref[b : b + 1, :] + lists[1, b]).astype(jnp.float32)
    done = pltpu.make_async_copy(out_ref, out_hbm, sem.at[0])
    done.start()
    done.wait()


def pack(turn, owner, pos, cell, cells_per, slots):
    blocks = owner.shape[1]
    return pl.pallas_call(
        functools.partial(pack_kernel, cells_per),
        name="pack",
        in_specs=[pl.BlockSpec(memory_space=pltpu.SMEM)] + [pl.BlockSpec(memory_space=pl.ANY)] * 3,
        out_specs=[pl.BlockSpec(memory_space=pl.ANY), pl.BlockSpec(memory_space=pltpu.VMEM)],
        out_shape=[
            jax.ShapeDtypeStruct((slots, 4, BLOCK), jnp.float32),
            jax.ShapeDtypeStruct((1, blocks), jnp.int32),
        ],
        scratch_shapes=[
            pltpu.VMEM(owner.shape, jnp.int32),
            pltpu.VMEM(pos.shape, jnp.float32),
            pltpu.VMEM(cell.shape, jnp.int32),
            pltpu.VMEM((slots, 4, BLOCK), jnp.float32),
            pltpu.VMEM((2, blocks), jnp.int32),
            pltpu.SMEM((2, blocks), jnp.int32),
            pltpu.SemaphoreType.DMA((4,)),
        ],
        compiler_params=pltpu.CompilerParams(vmem_limit_bytes=56 << 20),
    )(turn, owner, pos, cell)


CHUNK = 2048
ROOM = 4


def table_kernel(geom_ref, vals_ref, geom_two, vals_two, out_ref):
    for at in range(0, CHUNK, BLOCK):
        parts = [ref[:, at : at + BLOCK] for ref in (geom_ref, vals_ref, geom_two, vals_two)]
        out_ref[at : at + BLOCK, :] = jnp.concatenate(parts, axis=0).T


def table(geom, vals, geom_two, vals_two):
    cells = geom.shape[1]
    spot = lambda i: (0, i)
    return pl.pallas_call(
        table_kernel,
        name="table",
        grid=(cells // CHUNK,),
        in_specs=[
            pl.BlockSpec((24, CHUNK), spot),
            pl.BlockSpec((40, CHUNK), spot),
            pl.BlockSpec((24, CHUNK), spot),
            pl.BlockSpec((40, CHUNK), spot),
        ],
        out_specs=pl.BlockSpec((CHUNK, 2 * FIELDS), lambda i: (i, 0)),
        out_shape=jax.ShapeDtypeStruct((ROOM * cells, 2 * FIELDS), jnp.float32),
        compiler_params=pltpu.CompilerParams(vmem_limit_bytes=40 << 20),
        cost_estimate=pl.CostEstimate(flops=2 << 30, bytes_accessed=32 << 20, transcendentals=0),
    )(geom, vals, geom_two, vals_two)


GROUP = 8
READY = 6
AHEAD = 4


def cross(a, b):
    return (a[1] * b[2] - a[2] * b[1], a[2] * b[0] - a[0] * b[2], a[0] * b[1] - a[1] * b[0])


def dot3(a, b):
    return a[0] * b[0] + a[1] * b[1] + a[2] * b[2]


def newton_values(field, pos):
    geom = [[field(c * 8 + m) for m in range(8)] for c in range(3)]
    x = y = z = None
    for step in range(NEWTON):
        if step == 0:
            misfit = [geom[c][0] - pos[c] for c in range(3)]
            cols = [[geom[c][d + 1] for c in range(3)] for d in range(3)]
        else:
            xy, xz, yz = x * y, x * z, y * z
            misfit, cols = [], [[], [], []]
            for c in range(3):
                g = geom[c]
                dx = g[1] + y * g[4] + z * g[5] + yz * g[7]
                dy = g[2] + x * g[4] + z * g[6] + xz * g[7]
                dz = g[3] + x * g[5] + y * g[6] + xy * g[7]
                misfit.append((g[0] - pos[c]) + x * dx + y * (g[2] + z * g[6]) + z * g[3])
                cols[0].append(dx)
                cols[1].append(dy)
                cols[2].append(dz)
        bc, ca, ab = cross(cols[1], cols[2]), cross(cols[2], cols[0]), cross(cols[0], cols[1])
        determ = dot3(cols[0], bc)
        deltas = [dot3(misfit, side) / determ for side in (bc, ca, ab)]
        if step == 0:
            x, y, z = -deltas[0], -deltas[1], -deltas[2]
        else:
            x, y, z = x - deltas[0], y - deltas[1], z - deltas[2]
    xy, xz, yz = x * y, x * z, y * z
    xyz = xy * z
    results = []
    for k in range(VARS):
        h = [field(24 + k * 8 + m) for m in range(8)]
        results.append(
            (h[0] + x * h[1]) + (y * h[2] + z * h[3]) + (xy * h[4] + xz * h[5]) + (yz * h[6] + xyz * h[7])
        )
    return results


def main_kernel(recv, tab_hbm, mono, out, tab, marks, order, sets, sem):
    devices = recv.shape[0] // (4 * CAP)
    cells_per = tab.shape[0]
    fetch = pltpu.make_async_copy(tab_hbm.at[pl.ds(0, cells_per), :], tab, sem.at[3])
    fetch.start()
    sub = lax.broadcasted_iota(jnp.int32, (8, BLOCK), 0)
    lane = lax.broadcasted_iota(jnp.int32, (8, BLOCK), 1)
    count = jnp.zeros((devices, BLOCK), jnp.float32)
    for s in range(CAP):
        lead = recv[pl.ds(4 * s + 3, devices, stride=4 * CAP), :][:, 0:1]
        count = count + jnp.where(jnp.broadcast_to(lead, (devices, BLOCK)) >= 0.0, 1.0, 0.0)
    source = lax.broadcasted_iota(jnp.int32, (devices, devices), 0)
    other = lax.broadcasted_iota(jnp.int32, (devices, devices), 1)
    lower = jnp.where(other < source, 1.0, 0.0)
    start = jnp.dot(lower, count, preferred_element_type=jnp.float32)
    base = lax.broadcasted_iota(jnp.int32, (devices, BLOCK), 0).astype(jnp.float32) * CAP
    column = lax.broadcasted_iota(jnp.int32, (devices, BLOCK), 1).astype(jnp.float32) - 1.0
    ahead = column * GROUP - start
    for k in range(GROUP):
        turn = ahead + float(k)
        slot = jnp.where((turn >= 0.0) & (turn < count), base + turn, 0.0)
        marks[k : k + 1, :] = jnp.sum(slot, axis=0, keepdims=True).astype(jnp.int32)
    marks[8:9, :] = jnp.sum(count, axis=0, keepdims=True).astype(jnp.int32)
    copy = pltpu.make_async_copy(marks, order, sem.at[2])
    copy.start()
    copy.wait()
    total = order[8, 0]
    pairs = (total + 2 * GROUP - 1) // (2 * GROUP)
    masks = [sub == s for s in range(8)]

    def index_copy(p):
        return pltpu.make_async_copy(sets[p]["whole"], sets[p]["index"], sem.at[p])

    def stage(g, p):
        inbox = sets[p]["inbox"]
        for k in range(GROUP):
            e = order[k, g + 1]
            inbox[pl.ds(k, 4, stride=8), :] = recv[pl.ds(pl.multiple_of(e * 4, 4), 4), :]
        cell = jnp.maximum(inbox[24:32, :], 0.0).astype(jnp.int32)
        sets[p]["whole"][...] = jnp.where(cell >= cells_per, cell - cells_per, cell)

    def row(i):
        return jnp.broadcast_to(tab[pl.ds(i, 1), :], (8, 2 * FIELDS))

    def look(p, k, ready):
        index, inbox = sets[p]["index"], sets[p]["inbox"]
        theirs = jnp.broadcast_to(inbox[24 + k : 25 + k, :], (8, BLOCK)) >= float(cells_per)
        keep = (theirs == (lane >= FIELDS)) & ready
        for u in range(0, BLOCK, 16):
            tiles = []
            for h in (u, u + 8):
                tile = row(index[k, h])
                for s in range(1, 8):
                    tile = jnp.where(masks[s], row(index[k, h + s]), tile)
                tiles.append(jnp.where(keep, tile, 0.0))
            full = jnp.concatenate(tiles, axis=0)
            upper = full.astype(jnp.bfloat16)
            at = k * BLOCK + u
            sets[p]["rows"][at : at + 16, : 2 * FIELDS] = upper
            sets[p]["rows"][at : at + 16, 2 * FIELDS :] = (full - upper.astype(jnp.float32)).astype(jnp.bfloat16)

    def product(p, k):
        made = lax.dot_general(
            mono[...], sets[p]["rows"][k * BLOCK : (k + 2) * BLOCK, :], NT, preferred_element_type=jnp.float32
        )
        sets[p]["coefs"][pl.ds(k, FIELDS, stride=8), :] = made[:, :BLOCK]
        sets[p]["coefs"][pl.ds(k + 1, FIELDS, stride=8), :] = made[:, BLOCK:]

    def solve(g, p):
        for k in range(AHEAD, GROUP, 2):
            product(p, k)
        coefs, results = sets[p]["coefs"], sets[p]["results"]
        pos = [sets[p]["pos"][c * 8 : c * 8 + 8, :] for c in range(3)]
        made = newton_values(lambda i: coefs[i * 8 : i * 8 + 8, :], pos)
        for v in range(VARS):
            results[v * 8 : v * 8 + 8, :] = made[v]
        for k in range(GROUP):
            e = order[k, g + 1]
            out[pl.ds(e * VARS, VARS), :] = results[pl.ds(k, VARS, stride=8), :]
        return (made[4] <= 0.0) | (made[4] > 0.0) | (made[4] != made[4])

    stage(0, 0)
    index_copy(0).start()
    stage(1, 1)
    fetch.wait()

    def two(i, carry):
        for p in range(2):
            g = 2 * i + p
            index_copy(1 - p).start()
            index_copy(p).wait()
            sets[p]["pos"][...] = sets[p]["inbox"][0:24, :]
            ready = solve(g - 1, 1 - p)
            for k in range(GROUP):
                look(p, k, ready if k >= READY else True)
                if k % 2 and k < AHEAD:
                    product(p, k - 1)
            stage(g + 2, p)
        return carry

    lax.fori_loop(0, pairs, two, 0)

    index_copy(0).wait()

    @pl.when(pairs > 0)
    def _():
        solve(2 * pairs - 1, 1)


def main_entry(recv, tab, mono, out, *scratch):
    names = ("inbox", "whole", "index", "pos", "rows", "coefs", "results")
    sets = [dict(zip(names, scratch[3 + 7 * p : 10 + 7 * p])) for p in range(2)]
    main_kernel(recv, tab, mono, out, *scratch[:3], sets, scratch[-1])


def main(recv, tab):
    entries = recv.shape[0] // 4
    devices = entries // CAP
    mono = jnp.asarray(monomial_matrix(), jnp.bfloat16)
    one_set = [
        pltpu.VMEM((32, BLOCK), jnp.float32),
        pltpu.VMEM((8, BLOCK), jnp.int32),
        pltpu.SMEM((8, BLOCK), jnp.int32),
        pltpu.VMEM((24, BLOCK), jnp.float32),
        pltpu.VMEM((GROUP * BLOCK, 4 * FIELDS), jnp.bfloat16),
        pltpu.VMEM((8 * FIELDS, BLOCK), jnp.float32),
        pltpu.VMEM((8 * VARS, BLOCK), jnp.float32),
    ]
    return pl.pallas_call(
        main_entry,
        name="main",
        in_specs=[
            pl.BlockSpec(memory_space=pltpu.VMEM),
            pl.BlockSpec(memory_space=pl.ANY),
            pl.BlockSpec(memory_space=pltpu.VMEM),
        ],
        out_specs=pl.BlockSpec(memory_space=pltpu.VMEM),
        out_shape=jax.ShapeDtypeStruct((entries * VARS, BLOCK), jnp.float32),
        scratch_shapes=[
            pltpu.VMEM((tab.shape[0] // ROOM, tab.shape[1]), jnp.float32),
            pltpu.VMEM((16, BLOCK), jnp.int32),
            pltpu.SMEM((16, BLOCK), jnp.int32),
            *one_set,
            *one_set,
            pltpu.SemaphoreType.DMA((4,)),
        ],
        compiler_params=pltpu.CompilerParams(vmem_limit_bytes=40 << 20),
        cost_estimate=pl.CostEstimate(flops=2 << 30, bytes_accessed=20 << 20, transcendentals=0),
    )(recv, tab, mono)


def unpack_kernel(place_ref, answers, out_ref):
    blocks = place_ref.shape[1]

    for b in range(blocks):
        out_ref[:, b * BLOCK : (b + 1) * BLOCK] = answers[pl.ds(place_ref[0, b], VARS), :]


def unpack(place, answers):
    blocks = place.shape[1]
    return pl.pallas_call(
        unpack_kernel,
        name="unpack",
        in_specs=[pl.BlockSpec(memory_space=pltpu.SMEM), pl.BlockSpec(memory_space=pltpu.VMEM)],
        out_specs=pl.BlockSpec(memory_space=pltpu.VMEM),
        out_shape=jax.ShapeDtypeStruct((VARS, blocks * BLOCK), jnp.float32),
        compiler_params=pltpu.CompilerParams(vmem_limit_bytes=8 << 20),
    )(place, answers)


def per_device(recv_pos, donor_cell, block_owner, cell_geom, cell_values):
    devices = lax.axis_size(AXES)
    blocks = block_owner.shape[0]
    cells_per = cell_geom.shape[1]
    slots = devices * CAP
    swap = [(i, i ^ 1) for i in range(lax.axis_size("brick"))]
    geom_two = lax.ppermute(cell_geom, "brick", swap)
    vals_two = lax.ppermute(cell_values, "brick", swap)
    turn = (lax.axis_index("brick") >> 1 & 1).astype(jnp.int32)[None]
    outgoing, place = pack(
        turn, block_owner.reshape(1, blocks), recv_pos, donor_cell.reshape(blocks, BLOCK), cells_per, slots
    )
    arrived = lax.all_to_all(
        outgoing.reshape(devices, CAP, 4, BLOCK), AXES, split_axis=0, concat_axis=0, tiled=True
    )
    tab = table(cell_geom, cell_values, geom_two, vals_two)
    answer = main(arrived.reshape(slots * 4, BLOCK), tab)
    answers = lax.all_to_all(
        answer.reshape(devices, VARS, CAP, BLOCK), AXES, split_axis=0, concat_axis=0, tiled=True
    )
    return unpack(place, answers.reshape(slots * VARS, BLOCK))


def solution(mesh):
    placed = (
        P(None, AXES),
        P(AXES),
        P(AXES, None),
        P(None, AXES),
        P(None, AXES),
    )
    return jax.shard_map(
        per_device,
        mesh=mesh,
        in_specs=placed,
        out_specs=P(None, AXES),
        check_vma=False,
    )
```

```python
import functools

import jax
import jax.numpy as jnp
from jax import lax
from jax.experimental import pallas as pl
from jax.experimental.pallas import tpu as pltpu
from jax.sharding import PartitionSpec as P

BLOCK = 128
CAP = 4
NEWTON = 3
VARS = 5
FIELDS = 64
AXES = ("near", "brick")


def pack_kernel(cells_per, turn_ref, owner_hbm, pos_hbm, cell_hbm, out_hbm, place_ref, owner_ref, pos_ref, cell_ref, out_ref, spot, lists, sem):
    blocks = owner_ref.shape[1]
    fetches = [
        pltpu.make_async_copy(source, target, sem.at[i])
        for i, (source, target) in enumerate(((owner_hbm, owner_ref), (pos_hbm, pos_ref), (cell_hbm, cell_ref)))
    ]
    for fetch in fetches:
        fetch.start()
    out_ref[...] = jnp.full(out_ref.shape, -1.0, jnp.float32)
    fetches[0].wait()
    owner = owner_ref[...]
    key = jnp.broadcast_to((owner >> 1).astype(jnp.float32), (blocks, blocks))
    earlier = lax.broadcasted_iota(jnp.int32, (blocks, blocks), 0)
    later = lax.broadcasted_iota(jnp.int32, (blocks, blocks), 1)
    same = jnp.where((key.T == key) & (earlier < later), 1.0, 0.0)
    rank = jnp.sum(same, axis=0, keepdims=True).astype(jnp.int32)
    core = (rank + turn_ref[0]) & 1
    place = ((owner & -2) + core) * CAP + (rank >> 1)
    place_ref[...] = place * VARS
    spot[0:1, :] = place
    spot[1:2, :] = ((owner ^ core) & 1) * cells_per
    copy = pltpu.make_async_copy(spot, lists, sem.at[3])
    copy.start()
    copy.wait()
    fetches[1].wait()
    fetches[2].wait()

    for b in range(blocks):
        e = lists[0, b]
        out_ref[e, 0:3, :] = pos_ref[:, b * BLOCK : (b + 1) * BLOCK]
        out_ref[e, 3:4, :] = (cell_ref[b : b + 1, :] + lists[1, b]).astype(jnp.float32)
    done = pltpu.make_async_copy(out_ref, out_hbm, sem.at[0])
    done.start()
    done.wait()


def pack(turn, owner, pos, cell, cells_per, slots):
    blocks = owner.shape[1]
    return pl.pallas_call(
        functools.partial(pack_kernel, cells_per),
        name="pack",
        in_specs=[pl.BlockSpec(memory_space=pltpu.SMEM)] + [pl.BlockSpec(memory_space=pl.ANY)] * 3,
        out_specs=[pl.BlockSpec(memory_space=pl.ANY), pl.BlockSpec(memory_space=pltpu.VMEM)],
        out_shape=[
            jax.ShapeDtypeStruct((slots, 4, BLOCK), jnp.float32),
            jax.ShapeDtypeStruct((1, blocks), jnp.int32),
        ],
        scratch_shapes=[
            pltpu.VMEM(owner.shape, jnp.int32),
            pltpu.VMEM(pos.shape, jnp.float32),
            pltpu.VMEM(cell.shape, jnp.int32),
            pltpu.VMEM((slots, 4, BLOCK), jnp.float32),
            pltpu.VMEM((2, blocks), jnp.int32),
            pltpu.SMEM((2, blocks), jnp.int32),
            pltpu.SemaphoreType.DMA((4,)),
        ],
        compiler_params=pltpu.CompilerParams(vmem_limit_bytes=56 << 20),
    )(turn, owner, pos, cell)


CHUNK = 2048
ROOM = 4


def table_kernel(geom_ref, vals_ref, geom_two, vals_two, out_ref):
    for at in range(0, CHUNK, BLOCK):
        parts = [ref[:, at : at + BLOCK] for ref in (geom_ref, vals_ref, geom_two, vals_two)]
        out_ref[at : at + BLOCK, :] = jnp.concatenate(parts, axis=0).T


def table(geom, vals, geom_two, vals_two):
    cells = geom.shape[1]
    spot = lambda i: (0, i)
    return pl.pallas_call(
        table_kernel,
        name="table",
        grid=(cells // CHUNK,),
        in_specs=[
            pl.BlockSpec((24, CHUNK), spot),
            pl.BlockSpec((40, CHUNK), spot),
            pl.BlockSpec((24, CHUNK), spot),
            pl.BlockSpec((40, CHUNK), spot),
        ],
        out_specs=pl.BlockSpec((CHUNK, 2 * FIELDS), lambda i: (i, 0)),
        out_shape=jax.ShapeDtypeStruct((ROOM * cells, 2 * FIELDS), jnp.float32),
        compiler_params=pltpu.CompilerParams(vmem_limit_bytes=40 << 20),
        cost_estimate=pl.CostEstimate(flops=2 << 30, bytes_accessed=32 << 20, transcendentals=0),
    )(geom, vals, geom_two, vals_two)


GROUP = 8
AHEAD = 6


def cross(a, b):
    return (a[1] * b[2] - a[2] * b[1], a[2] * b[0] - a[0] * b[2], a[0] * b[1] - a[1] * b[0])


def dot3(a, b):
    return a[0] * b[0] + a[1] * b[1] + a[2] * b[2]


def expand(corner):
    one = [corner[2 * j + 1] + corner[2 * j] for j in range(4)]
    ex = [corner[2 * j + 1] - corner[2 * j] for j in range(4)]
    pairs = [(t[1] + t[0], t[3] + t[2], t[1] - t[0], t[3] - t[2]) for t in (one, ex)]
    (c0, c1, y0, y1), (x0, x1, xy0, xy1) = pairs
    return (c1 + c0, x1 + x0, y1 + y0, c1 - c0, xy1 + xy0, x1 - x0, y1 - y0, xy1 - xy0)


def newton_values(field, pos):
    geom = [expand([field(c * 8 + v) for v in range(8)]) for c in range(3)]
    pos = [8.0 * p for p in pos]
    x = y = z = None
    for step in range(NEWTON):
        if step == 0:
            misfit = [geom[c][0] - pos[c] for c in range(3)]
            cols = [[geom[c][d + 1] for c in range(3)] for d in range(3)]
        else:
            xy, xz, yz = x * y, x * z, y * z
            misfit, cols = [], [[], [], []]
            for c in range(3):
                g = geom[c]
                dx = g[1] + y * g[4] + z * g[5] + yz * g[7]
                dy = g[2] + x * g[4] + z * g[6] + xz * g[7]
                dz = g[3] + x * g[5] + y * g[6] + xy * g[7]
                misfit.append((g[0] - pos[c]) + x * dx + y * (g[2] + z * g[6]) + z * g[3])
                cols[0].append(dx)
                cols[1].append(dy)
                cols[2].append(dz)
        bc, ca, ab = cross(cols[1], cols[2]), cross(cols[2], cols[0]), cross(cols[0], cols[1])
        determ = dot3(cols[0], bc)
        deltas = [dot3(misfit, side) / determ for side in (bc, ca, ab)]
        if step == 0:
            x, y, z = -deltas[0], -deltas[1], -deltas[2]
        else:
            x, y, z = x - deltas[0], y - deltas[1], z - deltas[2]
    xy, xz, yz = x * y, x * z, y * z
    xyz = xy * z
    results = []
    for k in range(VARS):
        h = expand([field(24 + k * 8 + v) for v in range(8)])
        total = (h[0] + x * h[1]) + (y * h[2] + z * h[3]) + (xy * h[4] + xz * h[5]) + (yz * h[6] + xyz * h[7])
        results.append(0.125 * total)
    return results


def main_kernel(recv, tab_hbm, out, tab, marks, order, sets, sem):
    devices = recv.shape[0] // (4 * CAP)
    cells_per = tab.shape[0]
    fetch = pltpu.make_async_copy(tab_hbm.at[pl.ds(0, cells_per), :], tab, sem.at[3])
    fetch.start()
    sub = lax.broadcasted_iota(jnp.int32, (8, BLOCK), 0)
    lane = lax.broadcasted_iota(jnp.int32, (8, BLOCK), 1)
    count = jnp.zeros((devices, BLOCK), jnp.float32)
    for s in range(CAP):
        lead = recv[pl.ds(4 * s + 3, devices, stride=4 * CAP), :][:, 0:1]
        count = count + jnp.where(jnp.broadcast_to(lead, (devices, BLOCK)) >= 0.0, 1.0, 0.0)
    source = lax.broadcasted_iota(jnp.int32, (devices, devices), 0)
    other = lax.broadcasted_iota(jnp.int32, (devices, devices), 1)
    lower = jnp.where(other < source, 1.0, 0.0)
    start = jnp.dot(lower, count, preferred_element_type=jnp.float32)
    base = lax.broadcasted_iota(jnp.int32, (devices, BLOCK), 0).astype(jnp.float32) * CAP
    column = lax.broadcasted_iota(jnp.int32, (devices, BLOCK), 1).astype(jnp.float32) - 1.0
    ahead = column * GROUP - start
    for k in range(GROUP):
        turn = ahead + float(k)
        slot = jnp.where((turn >= 0.0) & (turn < count), base + turn, 0.0)
        marks[k : k + 1, :] = jnp.sum(slot, axis=0, keepdims=True).astype(jnp.int32)
    marks[8:9, :] = jnp.sum(count, axis=0, keepdims=True).astype(jnp.int32)
    copy = pltpu.make_async_copy(marks, order, sem.at[2])
    copy.start()
    copy.wait()
    total = order[8, 0]
    pairs = (total + 2 * GROUP - 1) // (2 * GROUP)
    masks = [sub == s for s in range(8)]

    def index_copy(p):
        return pltpu.make_async_copy(sets[p]["whole"], sets[p]["index"], sem.at[p])

    def stage(g, p):
        inbox = sets[p]["inbox"]
        for k in range(GROUP):
            e = order[k, g + 1]
            inbox[pl.ds(k, 4, stride=8), :] = recv[pl.ds(pl.multiple_of(e * 4, 4), 4), :]
        cell = jnp.maximum(inbox[24:32, :], 0.0).astype(jnp.int32)
        sets[p]["whole"][...] = jnp.where(cell >= cells_per, cell - cells_per, cell)

    def row(i):
        return jnp.broadcast_to(tab[pl.ds(i, 1), :], (8, 2 * FIELDS))

    def look(p, k):
        index = sets[p]["index"]
        for u in range(0, BLOCK, 8):
            tile = row(index[k, u])
            for s in range(1, 8):
                tile = jnp.where(masks[s], row(index[k, u + s]), tile)
            sets[p]["rows"][k * BLOCK + u : k * BLOCK + u + 8, :] = tile

    def product(p, k):
        for j in (k, k + 1):
            full = sets[p]["rows"][j * BLOCK : (j + 1) * BLOCK, :].T
            theirs = sets[p]["pos"][24 + j : 25 + j, :] >= float(cells_per)
            half = jnp.where(jnp.broadcast_to(theirs, (FIELDS, BLOCK)), full[FIELDS:], full[:FIELDS])
            sets[p]["coefs"][pl.ds(j, FIELDS, stride=8), :] = half

    def solve(g, p):
        for k in range(AHEAD, GROUP, 2):
            product(p, k)
        coefs, results = sets[p]["coefs"], sets[p]["results"]
        pos = [sets[p]["pos"][c * 8 : c * 8 + 8, :] for c in range(3)]
        made = newton_values(lambda i: coefs[i * 8 : i * 8 + 8, :], pos)
        for v in range(VARS):
            results[v * 8 : v * 8 + 8, :] = made[v]
        for k in range(GROUP):
            e = order[k, g + 1]
            out[pl.ds(e * VARS, VARS), :] = results[pl.ds(k, VARS, stride=8), :]

    stage(0, 0)
    index_copy(0).start()
    stage(1, 1)
    fetch.wait()

    def two(i, carry):
        for p in range(2):
            g = 2 * i + p
            index_copy(1 - p).start()
            index_copy(p).wait()
            sets[p]["pos"][...] = sets[p]["inbox"][...]
            solve(g - 1, 1 - p)
            for k in range(GROUP):
                look(p, k)
                if k % 2 and k < AHEAD:
                    product(p, k - 1)
            stage(g + 2, p)
        return carry

    lax.fori_loop(0, pairs, two, 0)

    index_copy(0).wait()

    @pl.when(pairs > 0)
    def _():
        solve(2 * pairs - 1, 1)


def main_entry(recv, tab, out, *scratch):
    names = ("inbox", "whole", "index", "pos", "rows", "coefs", "results")
    sets = [dict(zip(names, scratch[3 + 7 * p : 10 + 7 * p])) for p in range(2)]
    main_kernel(recv, tab, out, *scratch[:3], sets, scratch[-1])


def main(recv, tab):
    entries = recv.shape[0] // 4
    devices = entries // CAP
    one_set = [
        pltpu.VMEM((32, BLOCK), jnp.float32),
        pltpu.VMEM((8, BLOCK), jnp.int32),
        pltpu.SMEM((8, BLOCK), jnp.int32),
        pltpu.VMEM((32, BLOCK), jnp.float32),
        pltpu.VMEM((GROUP * BLOCK, 2 * FIELDS), jnp.float32),
        pltpu.VMEM((8 * FIELDS, BLOCK), jnp.float32),
        pltpu.VMEM((8 * VARS, BLOCK), jnp.float32),
    ]
    return pl.pallas_call(
        main_entry,
        name="main",
        in_specs=[
            pl.BlockSpec(memory_space=pltpu.VMEM),
            pl.BlockSpec(memory_space=pl.ANY),
        ],
        out_specs=pl.BlockSpec(memory_space=pltpu.VMEM),
        out_shape=jax.ShapeDtypeStruct((entries * VARS, BLOCK), jnp.float32),
        scratch_shapes=[
            pltpu.VMEM((tab.shape[0] // ROOM, tab.shape[1]), jnp.float32),
            pltpu.VMEM((16, BLOCK), jnp.int32),
            pltpu.SMEM((16, BLOCK), jnp.int32),
            *one_set,
            *one_set,
            pltpu.SemaphoreType.DMA((4,)),
        ],
        compiler_params=pltpu.CompilerParams(vmem_limit_bytes=40 << 20),
        cost_estimate=pl.CostEstimate(flops=2 << 30, bytes_accessed=20 << 20, transcendentals=0),
    )(recv, tab)


def unpack_kernel(place_ref, answers, out_ref):
    blocks = place_ref.shape[1]

    for b in range(blocks):
        out_ref[:, b * BLOCK : (b + 1) * BLOCK] = answers[pl.ds(place_ref[0, b], VARS), :]


def unpack(place, answers):
    blocks = place.shape[1]
    return pl.pallas_call(
        unpack_kernel,
        name="unpack",
        in_specs=[pl.BlockSpec(memory_space=pltpu.SMEM), pl.BlockSpec(memory_space=pltpu.VMEM)],
        out_specs=pl.BlockSpec(memory_space=pltpu.VMEM),
        out_shape=jax.ShapeDtypeStruct((VARS, blocks * BLOCK), jnp.float32),
        compiler_params=pltpu.CompilerParams(vmem_limit_bytes=8 << 20),
    )(place, answers)


def per_device(recv_pos, donor_cell, block_owner, cell_geom, cell_values):
    devices = lax.axis_size(AXES)
    blocks = block_owner.shape[0]
    cells_per = cell_geom.shape[1]
    slots = devices * CAP
    swap = [(i, i ^ 1) for i in range(lax.axis_size("brick"))]
    geom_two = lax.ppermute(cell_geom, "brick", swap)
    vals_two = lax.ppermute(cell_values, "brick", swap)
    turn = (lax.axis_index("brick") >> 1 & 1).astype(jnp.int32)[None]
    outgoing, place = pack(
        turn, block_owner.reshape(1, blocks), recv_pos, donor_cell.reshape(blocks, BLOCK), cells_per, slots
    )
    arrived = lax.all_to_all(
        outgoing.reshape(devices, CAP, 4, BLOCK), AXES, split_axis=0, concat_axis=0, tiled=True
    )
    tab = table(cell_geom, cell_values, geom_two, vals_two)
    answer = main(arrived.reshape(slots * 4, BLOCK), tab)
    answers = lax.all_to_all(
        answer.reshape(devices, VARS, CAP, BLOCK), AXES, split_axis=0, concat_axis=0, tiled=True
    )
    return unpack(place, answers.reshape(slots * VARS, BLOCK))


def solution(mesh):
    placed = (
        P(None, AXES),
        P(AXES),
        P(AXES, None),
        P(None, AXES),
        P(None, AXES),
    )
    return jax.shard_map(
        per_device,
        mesh=mesh,
        in_specs=placed,
        out_specs=P(None, AXES),
        check_vma=False,
    )
```

```python
import functools

import jax
import jax.numpy as jnp
from jax import lax
from jax.experimental import pallas as pl
from jax.experimental.pallas import tpu as pltpu
from jax.sharding import PartitionSpec as P

BLOCK = 128
CAP = 4
NEWTON = 3
VARS = 5
FIELDS = 64
AXES = ("near", "brick")


def pack_kernel(
    cells_per, owner_hbm, pos_hbm, cell_hbm, out_hbm, place_hbm, owner_ref, pos_ref, cell_ref, out_ref, place_ref, spot, lists, sem
):
    blocks = owner_ref.shape[1]
    fetches = [
        pltpu.make_async_copy(source, target, sem.at[i])
        for i, (source, target) in enumerate(((owner_hbm, owner_ref), (pos_hbm, pos_ref), (cell_hbm, cell_ref)))
    ]
    for fetch in fetches:
        fetch.start()
    out_ref[...] = jnp.full(out_ref.shape, -1.0, jnp.float32)
    fetches[0].wait()
    owner = owner_ref[...]
    key = jnp.broadcast_to((owner >> 1).astype(jnp.float32), (blocks, blocks))
    earlier = lax.broadcasted_iota(jnp.int32, (blocks, blocks), 0)
    later = lax.broadcasted_iota(jnp.int32, (blocks, blocks), 1)
    same = jnp.where((key.T == key) & (earlier < later), 1.0, 0.0)
    rank = jnp.sum(same, axis=0, keepdims=True).astype(jnp.int32)
    turn = jnp.broadcast_to(owner[:, 0:1] >> 1, owner.shape)
    core = (rank + turn) & 1
    place = ((owner & -2) + core) * CAP + (rank >> 1)
    place_ref[...] = place * VARS
    spot[0:1, :] = place
    spot[1:2, :] = ((owner ^ core) & 1) * cells_per
    copy = pltpu.make_async_copy(spot, lists, sem.at[3])
    copy.start()
    places = pltpu.make_async_copy(place_ref, place_hbm, sem.at[4])
    places.start()
    copy.wait()
    fetches[1].wait()
    fetches[2].wait()

    for b in range(blocks):
        e = lists[0, b]
        out_ref[e, 0:3, :] = pos_ref[:, b * BLOCK : (b + 1) * BLOCK]
        out_ref[e, 3:4, :] = (cell_ref[b : b + 1, :] + lists[1, b]).astype(jnp.float32)
    done = pltpu.make_async_copy(out_ref, out_hbm, sem.at[0])
    done.start()
    places.wait()
    done.wait()


def pack(owner, pos, cell, cells_per, slots):
    blocks = owner.shape[1]
    return pl.pallas_call(
        functools.partial(pack_kernel, cells_per),
        name="pack",
        in_specs=[pl.BlockSpec(memory_space=pl.ANY)] * 3,
        out_specs=[pl.BlockSpec(memory_space=pl.ANY)] * 2,
        out_shape=[
            jax.ShapeDtypeStruct((slots, 4, BLOCK), jnp.float32),
            jax.ShapeDtypeStruct((1, blocks), jnp.int32),
        ],
        scratch_shapes=[
            pltpu.VMEM(owner.shape, jnp.int32),
            pltpu.VMEM(pos.shape, jnp.float32),
            pltpu.VMEM(cell.shape, jnp.int32),
            pltpu.VMEM((slots, 4, BLOCK), jnp.float32),
            pltpu.VMEM((1, blocks), jnp.int32),
            pltpu.VMEM((2, blocks), jnp.int32),
            pltpu.SMEM((2, blocks), jnp.int32),
            pltpu.SemaphoreType.DMA((5,)),
        ],
        compiler_params=pltpu.CompilerParams(vmem_limit_bytes=56 << 20),
    )(owner, pos, cell)


CHUNK = 2048
ROOM = 4


def table_kernel(geom_ref, vals_ref, geom_two, vals_two, out_ref):
    for at in range(0, CHUNK, BLOCK):
        parts = [ref[:, at : at + BLOCK] for ref in (geom_ref, vals_ref, geom_two, vals_two)]
        out_ref[at : at + BLOCK, :] = jnp.concatenate(parts, axis=0).T


def table(geom, vals, geom_two, vals_two):
    cells = geom.shape[1]
    spot = lambda i: (0, i)
    return pl.pallas_call(
        table_kernel,
        name="table",
        grid=(cells // CHUNK,),
        in_specs=[
            pl.BlockSpec((24, CHUNK), spot),
            pl.BlockSpec((40, CHUNK), spot),
            pl.BlockSpec((24, CHUNK), spot),
            pl.BlockSpec((40, CHUNK), spot),
        ],
        out_specs=pl.BlockSpec((CHUNK, 2 * FIELDS), lambda i: (i, 0)),
        out_shape=jax.ShapeDtypeStruct((ROOM * cells, 2 * FIELDS), jnp.float32),
        compiler_params=pltpu.CompilerParams(vmem_limit_bytes=40 << 20),
        cost_estimate=pl.CostEstimate(flops=2 << 30, bytes_accessed=32 << 20, transcendentals=0),
    )(geom, vals, geom_two, vals_two)


GROUP = 8
AHEAD = 6


def cross(a, b):
    return (a[1] * b[2] - a[2] * b[1], a[2] * b[0] - a[0] * b[2], a[0] * b[1] - a[1] * b[0])


def dot3(a, b):
    return a[0] * b[0] + a[1] * b[1] + a[2] * b[2]


def expand(corner):
    one = [corner[2 * j + 1] + corner[2 * j] for j in range(4)]
    ex = [corner[2 * j + 1] - corner[2 * j] for j in range(4)]
    pairs = [(t[1] + t[0], t[3] + t[2], t[1] - t[0], t[3] - t[2]) for t in (one, ex)]
    (c0, c1, y0, y1), (x0, x1, xy0, xy1) = pairs
    return (c1 + c0, x1 + x0, y1 + y0, c1 - c0, xy1 + xy0, x1 - x0, y1 - y0, xy1 - xy0)


def newton_values(field, pos):
    geom = [expand([field(c * 8 + v) for v in range(8)]) for c in range(3)]
    pos = [8.0 * p for p in pos]
    x = y = z = None
    for step in range(NEWTON):
        if step == 0:
            misfit = [geom[c][0] - pos[c] for c in range(3)]
            cols = [[geom[c][d + 1] for c in range(3)] for d in range(3)]
        else:
            xy, xz, yz = x * y, x * z, y * z
            misfit, cols = [], [[], [], []]
            for c in range(3):
                g = geom[c]
                dx = g[1] + y * g[4] + z * g[5] + yz * g[7]
                dy = g[2] + x * g[4] + z * g[6] + xz * g[7]
                dz = g[3] + x * g[5] + y * g[6] + xy * g[7]
                misfit.append((g[0] - pos[c]) + x * dx + y * (g[2] + z * g[6]) + z * g[3])
                cols[0].append(dx)
                cols[1].append(dy)
                cols[2].append(dz)
        bc, ca, ab = cross(cols[1], cols[2]), cross(cols[2], cols[0]), cross(cols[0], cols[1])
        determ = dot3(cols[0], bc)
        deltas = [dot3(misfit, side) / determ for side in (bc, ca, ab)]
        if step == 0:
            x, y, z = -deltas[0], -deltas[1], -deltas[2]
        else:
            x, y, z = x - deltas[0], y - deltas[1], z - deltas[2]
    xy, xz, yz = x * y, x * z, y * z
    xyz = xy * z
    results = []
    for k in range(VARS):
        h = expand([field(24 + k * 8 + v) for v in range(8)])
        total = (h[0] + x * h[1]) + (y * h[2] + z * h[3]) + (xy * h[4] + xz * h[5]) + (yz * h[6] + xyz * h[7])
        results.append(0.125 * total)
    return results


def main_kernel(recv, tab_hbm, out, tab, marks, order, sets, sem):
    devices = recv.shape[0] // (4 * CAP)
    cells_per = tab.shape[0]
    fetch = pltpu.make_async_copy(tab_hbm.at[pl.ds(0, cells_per), :], tab, sem.at[3])
    fetch.start()
    sub = lax.broadcasted_iota(jnp.int32, (8, BLOCK), 0)
    lane = lax.broadcasted_iota(jnp.int32, (8, BLOCK), 1)
    count = jnp.zeros((devices, BLOCK), jnp.float32)
    for s in range(CAP):
        lead = recv[pl.ds(4 * s + 3, devices, stride=4 * CAP), :][:, 0:1]
        count = count + jnp.where(jnp.broadcast_to(lead, (devices, BLOCK)) >= 0.0, 1.0, 0.0)
    source = lax.broadcasted_iota(jnp.int32, (devices, devices), 0)
    other = lax.broadcasted_iota(jnp.int32, (devices, devices), 1)
    lower = jnp.where(other < source, 1.0, 0.0)
    start = jnp.dot(lower, count, preferred_element_type=jnp.float32)
    base = lax.broadcasted_iota(jnp.int32, (devices, BLOCK), 0).astype(jnp.float32) * CAP
    column = lax.broadcasted_iota(jnp.int32, (devices, BLOCK), 1).astype(jnp.float32) - 1.0
    ahead = column * GROUP - start
    for k in range(GROUP):
        turn = ahead + float(k)
        slot = jnp.where((turn >= 0.0) & (turn < count), base + turn, 0.0)
        marks[k : k + 1, :] = jnp.sum(slot, axis=0, keepdims=True).astype(jnp.int32)
    marks[8:9, :] = jnp.sum(count, axis=0, keepdims=True).astype(jnp.int32)
    copy = pltpu.make_async_copy(marks, order, sem.at[2])
    copy.start()
    copy.wait()
    total = order[8, 0]
    groups = (total + GROUP - 1) // GROUP
    masks = [sub == s for s in range(8)]

    def index_copy(p):
        return pltpu.make_async_copy(sets[p]["whole"], sets[p]["index"], sem.at[p])

    def stage(g, p):
        inbox = sets[p]["inbox"]
        for k in range(GROUP):
            e = order[k, g + 1]
            inbox[pl.ds(k, 4, stride=8), :] = recv[pl.ds(pl.multiple_of(e * 4, 4), 4), :]
        cell = jnp.maximum(inbox[24:32, :], 0.0).astype(jnp.int32)
        sets[p]["whole"][...] = jnp.where(cell >= cells_per, cell - cells_per, cell)

    def row(i):
        return jnp.broadcast_to(tab[pl.ds(i, 1), :], (8, 2 * FIELDS))

    def look(p, k):
        index = sets[p]["index"]
        for u in range(0, BLOCK, 8):
            tile = row(index[k, u])
            for s in range(1, 8):
                tile = jnp.where(masks[s], row(index[k, u + s]), tile)
            sets[p]["rows"][k * BLOCK + u : k * BLOCK + u + 8, :] = tile

    def product(p, k):
        for j in (k, k + 1):
            full = sets[p]["rows"][j * BLOCK : (j + 1) * BLOCK, :].T
            theirs = sets[p]["pos"][24 + j : 25 + j, :] >= float(cells_per)
            half = jnp.where(jnp.broadcast_to(theirs, (FIELDS, BLOCK)), full[FIELDS:], full[:FIELDS])
            sets[p]["coefs"][pl.ds(j, FIELDS, stride=8), :] = half

    def solve(g, p):
        for k in range(AHEAD, GROUP, 2):
            product(p, k)
        coefs, results = sets[p]["coefs"], sets[p]["results"]
        pos = [sets[p]["pos"][c * 8 : c * 8 + 8, :] for c in range(3)]
        made = newton_values(lambda i: coefs[i * 8 : i * 8 + 8, :], pos)
        for v in range(VARS):
            results[v * 8 : v * 8 + 8, :] = made[v]
        for k in range(GROUP):
            e = order[k, g + 1]
            out[pl.ds(e * VARS, VARS), :] = results[pl.ds(k, VARS, stride=8), :]

    stage(0, 0)
    index_copy(0).start()
    stage(1, 1)
    fetch.wait()

    def group(g, p):
        sets[p]["pos"][...] = sets[p]["inbox"][...]
        solve(g - 1, 1 - p)
        for k in range(GROUP):
            look(p, k)
            if k % 2 and k < AHEAD:
                product(p, k - 1)

    def two(i, carry):
        for p in range(2):
            g = 2 * i + p
            index_copy(1 - p).start()
            index_copy(p).wait()
            group(g, p)
            stage(g + 2, p)
        return carry

    lax.fori_loop(0, groups >> 1, two, 0)
    index_copy(0).wait()
    last = groups & -2

    @pl.when(groups & 1 == 1)
    def _():
        group(last, 0)
        solve(last, 0)

    @pl.when((groups & 1 == 0) & (groups > 0))
    def _():
        solve(last - 1, 1)


def main_entry(recv, tab, out, *scratch):
    names = ("inbox", "whole", "index", "pos", "rows", "coefs", "results")
    sets = [dict(zip(names, scratch[3 + 7 * p : 10 + 7 * p])) for p in range(2)]
    main_kernel(recv, tab, out, *scratch[:3], sets, scratch[-1])


def main(recv, tab):
    entries = recv.shape[0] // 4
    devices = entries // CAP
    one_set = [
        pltpu.VMEM((32, BLOCK), jnp.float32),
        pltpu.VMEM((8, BLOCK), jnp.int32),
        pltpu.SMEM((8, BLOCK), jnp.int32),
        pltpu.VMEM((32, BLOCK), jnp.float32),
        pltpu.VMEM((GROUP * BLOCK, 2 * FIELDS), jnp.float32),
        pltpu.VMEM((8 * FIELDS, BLOCK), jnp.float32),
        pltpu.VMEM((8 * VARS, BLOCK), jnp.float32),
    ]
    return pl.pallas_call(
        main_entry,
        name="main",
        in_specs=[
            pl.BlockSpec(memory_space=pltpu.VMEM),
            pl.BlockSpec(memory_space=pl.ANY),
        ],
        out_specs=pl.BlockSpec(memory_space=pltpu.VMEM),
        out_shape=jax.ShapeDtypeStruct((entries * VARS, BLOCK), jnp.float32),
        scratch_shapes=[
            pltpu.VMEM((tab.shape[0] // ROOM, tab.shape[1]), jnp.float32),
            pltpu.VMEM((16, BLOCK), jnp.int32),
            pltpu.SMEM((16, BLOCK), jnp.int32),
            *one_set,
            *one_set,
            pltpu.SemaphoreType.DMA((4,)),
        ],
        compiler_params=pltpu.CompilerParams(vmem_limit_bytes=40 << 20),
        cost_estimate=pl.CostEstimate(flops=2 << 30, bytes_accessed=20 << 20, transcendentals=0),
    )(recv, tab)


PARTS = 4


def unpack_kernel(place_ref, answers, out_hbm, out_ref, sem):
    blocks = place_ref.shape[1]
    width = blocks * BLOCK // PARTS
    copies = []
    for b in range(blocks):
        out_ref[:, b * BLOCK : (b + 1) * BLOCK] = answers[pl.ds(place_ref[0, b], VARS), :]
        if (b + 1) * BLOCK % width == 0:
            part = pl.ds((b + 1) * BLOCK - width, width)
            copies.append(pltpu.make_async_copy(out_ref.at[:, part], out_hbm.at[:, part], sem.at[len(copies)]))
            copies[-1].start()
    for copy in copies:
        copy.wait()


def unpack(place, answers):
    blocks = place.shape[1]
    shape = (VARS, blocks * BLOCK)
    return pl.pallas_call(
        unpack_kernel,
        name="unpack",
        in_specs=[pl.BlockSpec(memory_space=pltpu.SMEM), pl.BlockSpec(memory_space=pltpu.VMEM)],
        out_specs=pl.BlockSpec(memory_space=pl.ANY),
        out_shape=jax.ShapeDtypeStruct(shape, jnp.float32),
        scratch_shapes=[pltpu.VMEM(shape, jnp.float32), pltpu.SemaphoreType.DMA((PARTS,))],
        compiler_params=pltpu.CompilerParams(vmem_limit_bytes=8 << 20),
    )(place, answers)


def per_device(recv_pos, donor_cell, block_owner, cell_geom, cell_values):
    devices = lax.axis_size(AXES)
    blocks = block_owner.shape[0]
    cells_per = cell_geom.shape[1]
    slots = devices * CAP
    swap = [(i, i ^ 1) for i in range(lax.axis_size("brick"))]
    geom_two = lax.ppermute(cell_geom, "brick", swap)
    vals_two = lax.ppermute(cell_values, "brick", swap)
    outgoing, place = pack(
        block_owner.reshape(1, blocks), recv_pos, donor_cell.reshape(blocks, BLOCK), cells_per, slots
    )
    arrived = lax.all_to_all(
        outgoing.reshape(devices, CAP, 4, BLOCK), AXES, split_axis=0, concat_axis=0, tiled=True
    )
    tab = table(cell_geom, cell_values, geom_two, vals_two)
    answer = main(arrived.reshape(slots * 4, BLOCK), tab)
    answers = lax.all_to_all(
        answer.reshape(devices, VARS, CAP, BLOCK), AXES, split_axis=0, concat_axis=0, tiled=True
    )
    return unpack(place, answers.reshape(slots * VARS, BLOCK))


def solution(mesh):
    placed = (
        P(None, AXES),
        P(AXES),
        P(AXES, None),
        P(None, AXES),
        P(None, AXES),
    )
    return jax.shard_map(
        per_device,
        mesh=mesh,
        in_specs=placed,
        out_specs=P(None, AXES),
        check_vma=False,
    )
```

```python
import functools

import jax
import jax.numpy as jnp
from jax import lax
from jax.experimental import pallas as pl
from jax.experimental.pallas import tpu as pltpu
from jax.sharding import PartitionSpec as P

BLOCK = 128
CAP = 4
NEWTON = 3
VARS = 5
FIELDS = 64
AXES = ("near", "brick")


def pack_kernel(
    cells_per, owner_hbm, pos_hbm, cell_hbm, out_hbm, place_hbm, owner_ref, pos_ref, cell_ref, out_ref, place_ref, spot, lists, sem
):
    blocks = owner_ref.shape[1]
    fetches = [
        pltpu.make_async_copy(source, target, sem.at[i])
        for i, (source, target) in enumerate(((owner_hbm, owner_ref), (pos_hbm, pos_ref), (cell_hbm, cell_ref)))
    ]
    for fetch in fetches:
        fetch.start()
    out_ref[...] = jnp.full(out_ref.shape, -1.0, jnp.float32)
    fetches[0].wait()
    owner = owner_ref[...]
    key = jnp.broadcast_to((owner >> 1).astype(jnp.float32), (blocks, blocks))
    earlier = lax.broadcasted_iota(jnp.int32, (blocks, blocks), 0)
    later = lax.broadcasted_iota(jnp.int32, (blocks, blocks), 1)
    same = jnp.where((key.T == key) & (earlier < later), 1.0, 0.0)
    rank = jnp.sum(same, axis=0, keepdims=True).astype(jnp.int32)
    turn = jnp.broadcast_to(owner[:, 0:1] >> 1, owner.shape)
    core = (rank + turn) & 1
    place = ((owner & -2) + core) * CAP + (rank >> 1)
    place_ref[...] = place * VARS
    spot[0:1, :] = place
    spot[1:2, :] = ((owner ^ core) & 1) * cells_per
    copy = pltpu.make_async_copy(spot, lists, sem.at[3])
    copy.start()
    places = pltpu.make_async_copy(place_ref, place_hbm, sem.at[4])
    places.start()
    copy.wait()
    fetches[1].wait()
    fetches[2].wait()

    for b in range(blocks):
        e = lists[0, b]
        out_ref[e, 0:3, :] = pos_ref[:, b * BLOCK : (b + 1) * BLOCK]
        out_ref[e, 3:4, :] = (cell_ref[b : b + 1, :] + lists[1, b]).astype(jnp.float32)
    done = pltpu.make_async_copy(out_ref, out_hbm, sem.at[0])
    done.start()
    places.wait()
    done.wait()


def pack(owner, pos, cell, cells_per, slots):
    blocks = owner.shape[1]
    return pl.pallas_call(
        functools.partial(pack_kernel, cells_per),
        name="pack",
        in_specs=[pl.BlockSpec(memory_space=pl.ANY)] * 3,
        out_specs=[pl.BlockSpec(memory_space=pl.ANY)] * 2,
        out_shape=[
            jax.ShapeDtypeStruct((slots, 4, BLOCK), jnp.float32),
            jax.ShapeDtypeStruct((1, blocks), jnp.int32),
        ],
        scratch_shapes=[
            pltpu.VMEM(owner.shape, jnp.int32),
            pltpu.VMEM(pos.shape, jnp.float32),
            pltpu.VMEM(cell.shape, jnp.int32),
            pltpu.VMEM((slots, 4, BLOCK), jnp.float32),
            pltpu.VMEM((1, blocks), jnp.int32),
            pltpu.VMEM((2, blocks), jnp.int32),
            pltpu.SMEM((2, blocks), jnp.int32),
            pltpu.SemaphoreType.DMA((5,)),
        ],
        compiler_params=pltpu.CompilerParams(vmem_limit_bytes=56 << 20),
    )(owner, pos, cell)


CHUNK = 2048
ROOM = 4


def table_kernel(steps, *refs):
    out_ref = refs[-1]

    def fill(parts):
        for at in range(0, CHUNK, BLOCK):
            tall = jnp.concatenate([ref[:, at : at + BLOCK] for ref in parts], axis=0)
            out_ref[at : at + BLOCK, :] = tall.T

    @pl.when(pl.program_id(0) < steps)
    def _():
        fill(refs[0:4])

    @pl.when(pl.program_id(0) >= steps)
    def _():
        fill(refs[4:8])


def table(geom, vals, geom_two, vals_two):
    cells = geom.shape[1]
    steps = cells // (2 * CHUNK)
    mine = [lambda i: (0, jnp.minimum(i, steps - 1)), lambda i: (0, steps + jnp.minimum(i, steps - 1))]
    others = [lambda i: (0, jnp.maximum(i - steps, 0)), lambda i: (0, steps + jnp.maximum(i - steps, 0))]
    return pl.pallas_call(
        functools.partial(table_kernel, steps),
        name="table",
        grid=(2 * steps,),
        in_specs=[pl.BlockSpec((rows, CHUNK), spot) for spots in (mine, others) for spot in spots for rows in (24, 40)],
        out_specs=pl.BlockSpec((CHUNK, 2 * FIELDS), lambda i: (i, 0)),
        out_shape=jax.ShapeDtypeStruct((ROOM * cells, 2 * FIELDS), jnp.float32),
        compiler_params=pltpu.CompilerParams(vmem_limit_bytes=40 << 20),
        cost_estimate=pl.CostEstimate(flops=2 << 30, bytes_accessed=32 << 20, transcendentals=0),
    )(geom, vals, geom, vals, geom_two, vals_two, geom_two, vals_two)


GROUP = 8
AHEAD = 6


def cross(a, b):
    return (a[1] * b[2] - a[2] * b[1], a[2] * b[0] - a[0] * b[2], a[0] * b[1] - a[1] * b[0])


def dot3(a, b):
    return a[0] * b[0] + a[1] * b[1] + a[2] * b[2]


def expand(corner):
    one = [corner[2 * j + 1] + corner[2 * j] for j in range(4)]
    ex = [corner[2 * j + 1] - corner[2 * j] for j in range(4)]
    pairs = [(t[1] + t[0], t[3] + t[2], t[1] - t[0], t[3] - t[2]) for t in (one, ex)]
    (c0, c1, y0, y1), (x0, x1, xy0, xy1) = pairs
    return (c1 + c0, x1 + x0, y1 + y0, c1 - c0, xy1 + xy0, x1 - x0, y1 - y0, xy1 - xy0)


def newton_values(field, pos):
    geom = [expand([field(c * 8 + v) for v in range(8)]) for c in range(3)]
    pos = [8.0 * p for p in pos]
    x = y = z = None
    for step in range(NEWTON):
        if step == 0:
            misfit = [geom[c][0] - pos[c] for c in range(3)]
            cols = [[geom[c][d + 1] for c in range(3)] for d in range(3)]
        else:
            xy, xz, yz = x * y, x * z, y * z
            misfit, cols = [], [[], [], []]
            for c in range(3):
                g = geom[c]
                dx = g[1] + y * g[4] + z * g[5] + yz * g[7]
                dy = g[2] + x * g[4] + z * g[6] + xz * g[7]
                dz = g[3] + x * g[5] + y * g[6] + xy * g[7]
                misfit.append((g[0] - pos[c]) + x * dx + y * (g[2] + z * g[6]) + z * g[3])
                cols[0].append(dx)
                cols[1].append(dy)
                cols[2].append(dz)
        bc, ca, ab = cross(cols[1], cols[2]), cross(cols[2], cols[0]), cross(cols[0], cols[1])
        determ = dot3(cols[0], bc)
        deltas = [dot3(misfit, side) / determ for side in (bc, ca, ab)]
        if step == 0:
            x, y, z = -deltas[0], -deltas[1], -deltas[2]
        else:
            x, y, z = x - deltas[0], y - deltas[1], z - deltas[2]
    xy, xz, yz = x * y, x * z, y * z
    xyz = xy * z
    results = []
    for k in range(VARS):
        h = expand([field(24 + k * 8 + v) for v in range(8)])
        total = (h[0] + x * h[1]) + (y * h[2] + z * h[3]) + (xy * h[4] + xz * h[5]) + (yz * h[6] + xyz * h[7])
        results.append(0.125 * total)
    return results


def main_kernel(recv, tab_hbm, out, tab, marks, order, sets, sem):
    devices = recv.shape[0] // (4 * CAP)
    cells_per = tab.shape[0]
    half = cells_per // 2
    fetches = [
        pltpu.make_async_copy(tab_hbm.at[pl.ds(i * half, half), :], tab.at[pl.ds(i * half, half), :], sem.at[3 + i])
        for i in range(2)
    ]
    fetches[0].start()
    sub = lax.broadcasted_iota(jnp.int32, (8, BLOCK), 0)
    lane = lax.broadcasted_iota(jnp.int32, (8, BLOCK), 1)
    zero = jnp.zeros((devices, BLOCK), jnp.float32)
    counts, found = [zero, zero], []
    for s in range(CAP):
        lead = recv[pl.ds(4 * s + 3, devices, stride=4 * CAP), :][:, 0:1]
        lead = jnp.broadcast_to(lead, (devices, BLOCK))
        here = [(lead >= 0.0) & (lead < float(cells_per)), lead >= float(cells_per)]
        found.append([(flag, count) for flag, count in zip(here, counts)])
        counts = [count + jnp.where(flag, 1.0, 0.0) for flag, count in zip(here, counts)]
    source = lax.broadcasted_iota(jnp.int32, (devices, devices), 0)
    other = lax.broadcasted_iota(jnp.int32, (devices, devices), 1)
    lower = jnp.where(other < source, 1.0, 0.0)
    sums = [jnp.sum(count, axis=0, keepdims=True) for count in counts]
    starts = [jnp.dot(lower, count, preferred_element_type=jnp.float32) for count in counts]
    starts[1] = starts[1] + sums[0]
    places = [
        jnp.where(mine[0], starts[0] + mine[1], jnp.where(theirs[0], starts[1] + theirs[1], -1024.0))
        for mine, theirs in found
    ]
    base = lax.broadcasted_iota(jnp.int32, (devices, BLOCK), 0).astype(jnp.float32) * CAP
    column = (lax.broadcasted_iota(jnp.int32, (devices, BLOCK), 1).astype(jnp.float32) - 1.0) * GROUP
    for k in range(GROUP):
        slot = zero
        for s in range(CAP):
            slot = jnp.where(places[s] == column + float(k), base + float(s), slot)
        marks[k : k + 1, :] = jnp.sum(slot, axis=0, keepdims=True).astype(jnp.int32)
    marks[8:9, :] = (sums[0] + sums[1]).astype(jnp.int32)
    marks[9:10, :] = sums[0].astype(jnp.int32)
    copy = pltpu.make_async_copy(marks, order, sem.at[2])
    copy.start()
    copy.wait()
    total = order[8, 0]
    groups = (total + GROUP - 1) // GROUP
    turning = order[9, 0] // (2 * GROUP)
    masks = [sub == s for s in range(8)]

    def index_copy(p):
        return pltpu.make_async_copy(sets[p]["whole"], sets[p]["index"], sem.at[p])

    def stage(g, p):
        inbox = sets[p]["inbox"]
        for k in range(GROUP):
            e = order[k, g + 1]
            inbox[pl.ds(k, 4, stride=8), :] = recv[pl.ds(pl.multiple_of(e * 4, 4), 4), :]
        cell = jnp.maximum(inbox[24:32, :], 0.0).astype(jnp.int32)
        theirs = cell >= cells_per
        cell = jnp.where(theirs, cell - cells_per, cell)
        cell = jnp.where(cell >= half, cell - half, cell)
        sets[p]["whole"][...] = jnp.where(theirs, cell + half, cell)

    def row(i):
        return jnp.broadcast_to(tab[pl.ds(i, 1), :], (8, 2 * FIELDS))

    def look(p, k):
        index = sets[p]["index"]
        for u in range(0, BLOCK, 8):
            tile = row(index[k, u])
            for s in range(1, 8):
                tile = jnp.where(masks[s], row(index[k, u + s]), tile)
            sets[p]["rows"][k * BLOCK + u : k * BLOCK + u + 8, :] = tile

    def product(p, k):
        for j in (k, k + 1):
            full = sets[p]["rows"][j * BLOCK : (j + 1) * BLOCK, :].T
            upper = jnp.broadcast_to(sets[p]["pos"][24 + j : 25 + j, :] > 0.0, (FIELDS, BLOCK))
            sets[p]["coefs"][pl.ds(j, FIELDS, stride=8), :] = jnp.where(upper, full[FIELDS:], full[:FIELDS])

    def solve(g, p):
        for k in range(AHEAD, GROUP, 2):
            product(p, k)
        coefs, results = sets[p]["coefs"], sets[p]["results"]
        pos = [sets[p]["pos"][c * 8 : c * 8 + 8, :] for c in range(3)]
        made = newton_values(lambda i: coefs[i * 8 : i * 8 + 8, :], pos)
        for v in range(VARS):
            results[v * 8 : v * 8 + 8, :] = made[v]
        for k in range(GROUP):
            e = order[k, g + 1]
            out[pl.ds(e * VARS, VARS), :] = results[pl.ds(k, VARS, stride=8), :]

    stage(0, 0)
    index_copy(0).start()
    stage(1, 1)

    def group(g, p):
        sets[p]["pos"][0:24, :] = sets[p]["inbox"][0:24, :]
        cell = sets[p]["inbox"][24:32, :]
        cell = jnp.where(cell >= float(cells_per), cell - float(cells_per), cell)
        sets[p]["pos"][24:32, :] = jnp.where(cell >= float(half), 1.0, 0.0)
        solve(g - 1, 1 - p)
        for k in range(GROUP):
            look(p, k)
            if k % 2 and k < AHEAD:
                product(p, k - 1)

    def two(i, carry):
        for p in range(2):
            g = 2 * i + p
            index_copy(1 - p).start()
            index_copy(p).wait()
            group(g, p)
            stage(g + 2, p)
        return carry

    def phase(part, carry):
        rows = pl.ds(pl.multiple_of(part * half, half), half)
        pltpu.make_async_copy(tab_hbm.at[rows, :], tab.at[rows, :], sem.at[3 + part]).wait()

        @pl.when(part == 0)
        def _():
            fetches[1].start()

        turn = jnp.minimum(turning, groups >> 1)
        lax.fori_loop(turn * part, jnp.where(part == 0, turn, groups >> 1), two, 0)
        return carry

    lax.fori_loop(0, 2, phase, 0)
    index_copy(0).wait()
    last = groups & -2

    @pl.when(groups & 1 == 1)
    def _():
        group(last, 0)
        solve(last, 0)

    @pl.when((groups & 1 == 0) & (groups > 0))
    def _():
        solve(last - 1, 1)


def main_entry(recv, tab, out, *scratch):
    names = ("inbox", "whole", "index", "pos", "rows", "coefs", "results")
    sets = [dict(zip(names, scratch[3 + 7 * p : 10 + 7 * p])) for p in range(2)]
    main_kernel(recv, tab, out, *scratch[:3], sets, scratch[-1])


def main(recv, tab):
    entries = recv.shape[0] // 4
    devices = entries // CAP
    one_set = [
        pltpu.VMEM((32, BLOCK), jnp.float32),
        pltpu.VMEM((8, BLOCK), jnp.int32),
        pltpu.SMEM((8, BLOCK), jnp.int32),
        pltpu.VMEM((32, BLOCK), jnp.float32),
        pltpu.VMEM((GROUP * BLOCK, 2 * FIELDS), jnp.float32),
        pltpu.VMEM((8 * FIELDS, BLOCK), jnp.float32),
        pltpu.VMEM((8 * VARS, BLOCK), jnp.float32),
    ]
    return pl.pallas_call(
        main_entry,
        name="main",
        in_specs=[
            pl.BlockSpec(memory_space=pltpu.VMEM),
            pl.BlockSpec(memory_space=pl.ANY),
        ],
        out_specs=pl.BlockSpec(memory_space=pltpu.VMEM),
        out_shape=jax.ShapeDtypeStruct((entries * VARS, BLOCK), jnp.float32),
        scratch_shapes=[
            pltpu.VMEM((tab.shape[0] // ROOM, tab.shape[1]), jnp.float32),
            pltpu.VMEM((16, BLOCK), jnp.int32),
            pltpu.SMEM((16, BLOCK), jnp.int32),
            *one_set,
            *one_set,
            pltpu.SemaphoreType.DMA((5,)),
        ],
        compiler_params=pltpu.CompilerParams(vmem_limit_bytes=40 << 20),
        cost_estimate=pl.CostEstimate(flops=2 << 30, bytes_accessed=20 << 20, transcendentals=0),
    )(recv, tab)


PARTS = 4


def unpack_kernel(place_ref, answers, out_hbm, out_ref, sem):
    blocks = place_ref.shape[1]
    width = blocks * BLOCK // PARTS
    copies = []
    for b in range(blocks):
        out_ref[:, b * BLOCK : (b + 1) * BLOCK] = answers[pl.ds(place_ref[0, b], VARS), :]
        if (b + 1) * BLOCK % width == 0:
            part = pl.ds((b + 1) * BLOCK - width, width)
            copies.append(pltpu.make_async_copy(out_ref.at[:, part], out_hbm.at[:, part], sem.at[len(copies)]))
            copies[-1].start()
    for copy in copies:
        copy.wait()


def unpack(place, answers):
    blocks = place.shape[1]
    shape = (VARS, blocks * BLOCK)
    return pl.pallas_call(
        unpack_kernel,
        name="unpack",
        in_specs=[pl.BlockSpec(memory_space=pltpu.SMEM), pl.BlockSpec(memory_space=pltpu.VMEM)],
        out_specs=pl.BlockSpec(memory_space=pl.ANY),
        out_shape=jax.ShapeDtypeStruct(shape, jnp.float32),
        scratch_shapes=[pltpu.VMEM(shape, jnp.float32), pltpu.SemaphoreType.DMA((PARTS,))],
        compiler_params=pltpu.CompilerParams(vmem_limit_bytes=8 << 20),
    )(place, answers)


def per_device(recv_pos, donor_cell, block_owner, cell_geom, cell_values):
    devices = lax.axis_size(AXES)
    blocks = block_owner.shape[0]
    cells_per = cell_geom.shape[1]
    slots = devices * CAP
    swap = [(i, i ^ 1) for i in range(lax.axis_size("brick"))]
    geom_two = lax.ppermute(cell_geom, "brick", swap)
    vals_two = lax.ppermute(cell_values, "brick", swap)
    outgoing, place = pack(
        block_owner.reshape(1, blocks), recv_pos, donor_cell.reshape(blocks, BLOCK), cells_per, slots
    )
    arrived = lax.all_to_all(
        outgoing.reshape(devices, CAP, 4, BLOCK), AXES, split_axis=0, concat_axis=0, tiled=True
    )
    tab = table(cell_geom, cell_values, geom_two, vals_two)
    answer = main(arrived.reshape(slots * 4, BLOCK), tab)
    answers = lax.all_to_all(
        answer.reshape(devices, VARS, CAP, BLOCK), AXES, split_axis=0, concat_axis=0, tiled=True
    )
    return unpack(place, answers.reshape(slots * VARS, BLOCK))


def solution(mesh):
    placed = (
        P(None, AXES),
        P(AXES),
        P(AXES, None),
        P(None, AXES),
        P(None, AXES),
    )
    return jax.shard_map(
        per_device,
        mesh=mesh,
        in_specs=placed,
        out_specs=P(None, AXES),
        check_vma=False,
    )
```

```python
import functools

import jax
import jax.numpy as jnp
from jax import lax
from jax.experimental import pallas as pl
from jax.experimental.pallas import tpu as pltpu
from jax.sharding import PartitionSpec as P

BLOCK = 128
CAP = 4
NEWTON = 3
VARS = 5
FIELDS = 64
AXES = ("near", "brick")


def pack_kernel(
    cells_per, owner_hbm, pos_hbm, cell_hbm, out_hbm, place_hbm, owner_ref, pos_ref, cell_ref, out_ref, place_ref, spot, lists, sem
):
    blocks = owner_ref.shape[1]
    fetches = [
        pltpu.make_async_copy(source, target, sem.at[i])
        for i, (source, target) in enumerate(((owner_hbm, owner_ref), (pos_hbm, pos_ref), (cell_hbm, cell_ref)))
    ]
    for fetch in fetches:
        fetch.start()
    out_ref[...] = jnp.full(out_ref.shape, -1.0, jnp.float32)
    fetches[0].wait()
    owner = owner_ref[...]
    key = jnp.broadcast_to((owner >> 1).astype(jnp.float32), (blocks, blocks))
    earlier = lax.broadcasted_iota(jnp.int32, (blocks, blocks), 0)
    later = lax.broadcasted_iota(jnp.int32, (blocks, blocks), 1)
    same = jnp.where((key.T == key) & (earlier < later), 1.0, 0.0)
    rank = jnp.sum(same, axis=0, keepdims=True).astype(jnp.int32)
    turn = jnp.broadcast_to(owner[:, 0:1] >> 1, owner.shape)
    core = (rank + turn) & 1
    place = ((owner & -2) + core) * CAP + (rank >> 1)
    place_ref[...] = place * VARS
    spot[0:1, :] = place
    spot[1:2, :] = ((owner ^ core) & 1) * cells_per
    copy = pltpu.make_async_copy(spot, lists, sem.at[3])
    copy.start()
    places = pltpu.make_async_copy(place_ref, place_hbm, sem.at[4])
    places.start()
    copy.wait()
    fetches[1].wait()
    fetches[2].wait()

    for b in range(blocks):
        e = lists[0, b]
        out_ref[e, 0:3, :] = pos_ref[:, b * BLOCK : (b + 1) * BLOCK]
        out_ref[e, 3:4, :] = (cell_ref[b : b + 1, :] + lists[1, b]).astype(jnp.float32)
    done = pltpu.make_async_copy(out_ref, out_hbm, sem.at[0])
    done.start()
    places.wait()
    done.wait()


def pack(owner, pos, cell, cells_per, slots):
    blocks = owner.shape[1]
    return pl.pallas_call(
        functools.partial(pack_kernel, cells_per),
        name="pack",
        in_specs=[pl.BlockSpec(memory_space=pl.ANY)] * 3,
        out_specs=[pl.BlockSpec(memory_space=pl.ANY)] * 2,
        out_shape=[
            jax.ShapeDtypeStruct((slots, 4, BLOCK), jnp.float32),
            jax.ShapeDtypeStruct((1, blocks), jnp.int32),
        ],
        scratch_shapes=[
            pltpu.VMEM(owner.shape, jnp.int32),
            pltpu.VMEM(pos.shape, jnp.float32),
            pltpu.VMEM(cell.shape, jnp.int32),
            pltpu.VMEM((slots, 4, BLOCK), jnp.float32),
            pltpu.VMEM((1, blocks), jnp.int32),
            pltpu.VMEM((2, blocks), jnp.int32),
            pltpu.SMEM((2, blocks), jnp.int32),
            pltpu.SemaphoreType.DMA((5,)),
        ],
        compiler_params=pltpu.CompilerParams(vmem_limit_bytes=56 << 20),
    )(owner, pos, cell)


CHUNK = 2048
ROOM = 4


def table_kernel(geom_ref, vals_ref, geom_two, vals_two, out_ref):
    for at in range(0, CHUNK, BLOCK):
        parts = [ref[:, at : at + BLOCK] for ref in (geom_ref, vals_ref, geom_two, vals_two)]
        out_ref[at : at + BLOCK, :] = jnp.concatenate(parts, axis=0).T


def table(geom, vals, geom_two, vals_two):
    cells = geom.shape[1]
    spot = lambda i: (0, i)
    return pl.pallas_call(
        table_kernel,
        name="table",
        grid=(cells // CHUNK,),
        in_specs=[
            pl.BlockSpec((24, CHUNK), spot),
            pl.BlockSpec((40, CHUNK), spot),
            pl.BlockSpec((24, CHUNK), spot),
            pl.BlockSpec((40, CHUNK), spot),
        ],
        out_specs=pl.BlockSpec((CHUNK, 2 * FIELDS), lambda i: (i, 0)),
        out_shape=jax.ShapeDtypeStruct((ROOM * cells, 2 * FIELDS), jnp.float32),
        compiler_params=pltpu.CompilerParams(vmem_limit_bytes=40 << 20),
        cost_estimate=pl.CostEstimate(flops=2 << 30, bytes_accessed=32 << 20, transcendentals=0),
    )(geom, vals, geom_two, vals_two)


GROUP = 8
AHEAD = 6


def cross(a, b):
    return (a[1] * b[2] - a[2] * b[1], a[2] * b[0] - a[0] * b[2], a[0] * b[1] - a[1] * b[0])


def dot3(a, b):
    return a[0] * b[0] + a[1] * b[1] + a[2] * b[2]


def expand(corner):
    one = [corner[2 * j + 1] + corner[2 * j] for j in range(4)]
    ex = [corner[2 * j + 1] - corner[2 * j] for j in range(4)]
    pairs = [(t[1] + t[0], t[3] + t[2], t[1] - t[0], t[3] - t[2]) for t in (one, ex)]
    (c0, c1, y0, y1), (x0, x1, xy0, xy1) = pairs
    return (c1 + c0, x1 + x0, y1 + y0, c1 - c0, xy1 + xy0, x1 - x0, y1 - y0, xy1 - xy0)


def newton_values(field, pos):
    geom = [expand([field(c * 8 + v) for v in range(8)]) for c in range(3)]
    pos = [8.0 * p for p in pos]
    x = y = z = None
    for step in range(NEWTON):
        if step == 0:
            misfit = [geom[c][0] - pos[c] for c in range(3)]
            cols = [[geom[c][d + 1] for c in range(3)] for d in range(3)]
        else:
            xy, xz, yz = x * y, x * z, y * z
            misfit, cols = [], [[], [], []]
            for c in range(3):
                g = geom[c]
                dx = g[1] + y * g[4] + z * g[5] + yz * g[7]
                dy = g[2] + x * g[4] + z * g[6] + xz * g[7]
                dz = g[3] + x * g[5] + y * g[6] + xy * g[7]
                misfit.append((g[0] - pos[c]) + x * dx + y * (g[2] + z * g[6]) + z * g[3])
                cols[0].append(dx)
                cols[1].append(dy)
                cols[2].append(dz)
        bc, ca, ab = cross(cols[1], cols[2]), cross(cols[2], cols[0]), cross(cols[0], cols[1])
        determ = dot3(cols[0], bc)
        deltas = [dot3(misfit, side) / determ for side in (bc, ca, ab)]
        if step == 0:
            x, y, z = -deltas[0], -deltas[1], -deltas[2]
        else:
            x, y, z = x - deltas[0], y - deltas[1], z - deltas[2]
    xy, xz, yz = x * y, x * z, y * z
    xyz = xy * z
    results = []
    for k in range(VARS):
        h = expand([field(24 + k * 8 + v) for v in range(8)])
        total = (h[0] + x * h[1]) + (y * h[2] + z * h[3]) + (xy * h[4] + xz * h[5]) + (yz * h[6] + xyz * h[7])
        results.append(0.125 * total)
    return results


def main_kernel(recv, tab_hbm, out, tab, marks, order, sets, sem):
    devices = recv.shape[0] // (4 * CAP)
    cells_per = tab.shape[0]
    fetch = pltpu.make_async_copy(tab_hbm.at[pl.ds(0, cells_per), :], tab, sem.at[3])
    fetch.start()
    sub = lax.broadcasted_iota(jnp.int32, (8, BLOCK), 0)
    lane = lax.broadcasted_iota(jnp.int32, (8, BLOCK), 1)
    count = jnp.zeros((devices, BLOCK), jnp.float32)
    for s in range(CAP):
        lead = recv[pl.ds(4 * s + 3, devices, stride=4 * CAP), :][:, 0:1]
        count = count + jnp.where(jnp.broadcast_to(lead, (devices, BLOCK)) >= 0.0, 1.0, 0.0)
    source = lax.broadcasted_iota(jnp.int32, (devices, devices), 0)
    other = lax.broadcasted_iota(jnp.int32, (devices, devices), 1)
    lower = jnp.where(other < source, 1.0, 0.0)
    start = jnp.dot(lower, count, preferred_element_type=jnp.float32)
    base = lax.broadcasted_iota(jnp.int32, (devices, BLOCK), 0).astype(jnp.float32) * CAP
    column = lax.broadcasted_iota(jnp.int32, (devices, BLOCK), 1).astype(jnp.float32) - 1.0
    ahead = column * GROUP - start
    for k in range(GROUP):
        turn = ahead + float(k)
        slot = jnp.where((turn >= 0.0) & (turn < count), base + turn, 0.0)
        slot = jnp.sum(slot, axis=0, keepdims=True).astype(jnp.int32)
        marks[k : k + 1, :] = slot * 4
        marks[16 + k : 17 + k, :] = slot * VARS
    marks[8:9, :] = jnp.sum(count, axis=0, keepdims=True).astype(jnp.int32)
    copy = pltpu.make_async_copy(marks, order, sem.at[2])
    copy.start()
    copy.wait()
    total = order[8, 0]
    groups = (total + GROUP - 1) // GROUP
    masks = [sub == s for s in range(8)]

    def index_copy(p):
        return pltpu.make_async_copy(sets[p]["whole"], sets[p]["index"], sem.at[p])

    def stage(g, p):
        inbox = sets[p]["inbox"]
        for k in range(GROUP):
            e = order[k, g + 1]
            inbox[pl.ds(k, 4, stride=8), :] = recv[pl.ds(pl.multiple_of(e, 4), 4), :]
        cell = jnp.maximum(inbox[24:32, :], 0.0).astype(jnp.int32)
        sets[p]["whole"][...] = jnp.where(cell >= cells_per, cell - cells_per, cell)

    def row(i):
        return jnp.broadcast_to(tab[pl.ds(i, 1), :], (8, 2 * FIELDS))

    def look(p, k):
        index = sets[p]["index"]
        for u in range(0, BLOCK, 8):
            tile = row(index[k, u])
            for s in range(1, 8):
                tile = jnp.where(masks[s], row(index[k, u + s]), tile)
            sets[p]["rows"][k * BLOCK + u : k * BLOCK + u + 8, :] = tile

    def product(p, k):
        for j in (k, k + 1):
            full = sets[p]["rows"][j * BLOCK : (j + 1) * BLOCK, :].T
            theirs = sets[p]["pos"][24 + j : 25 + j, :] >= float(cells_per)
            half = jnp.where(jnp.broadcast_to(theirs, (FIELDS, BLOCK)), full[FIELDS:], full[:FIELDS])
            sets[p]["coefs"][pl.ds(j, FIELDS, stride=8), :] = half

    def solve(g, p):
        for k in range(AHEAD, GROUP, 2):
            product(p, k)
        coefs, results = sets[p]["coefs"], sets[p]["results"]
        pos = [sets[p]["pos"][c * 8 : c * 8 + 8, :] for c in range(3)]
        made = newton_values(lambda i: coefs[i * 8 : i * 8 + 8, :], pos)
        for v in range(VARS):
            results[v * 8 : v * 8 + 8, :] = made[v]
        for k in range(GROUP):
            e = order[16 + k, g + 1]
            out[pl.ds(e, VARS), :] = results[pl.ds(k, VARS, stride=8), :]

    stage(0, 0)
    index_copy(0).start()
    stage(1, 1)
    fetch.wait()

    def group(g, p):
        sets[p]["pos"][...] = sets[p]["inbox"][...]
        solve(g - 1, 1 - p)
        for k in range(GROUP):
            look(p, k)
            if k % 2 and k < AHEAD:
                product(p, k - 1)

    def two(i, carry):
        for p in range(2):
            g = 2 * i + p
            index_copy(1 - p).start()
            index_copy(p).wait()
            group(g, p)
            stage(g + 2, p)
        return carry

    lax.fori_loop(0, groups >> 1, two, 0)
    index_copy(0).wait()
    last = groups & -2

    @pl.when(groups & 1 == 1)
    def _():
        group(last, 0)
        solve(last, 0)

    @pl.when((groups & 1 == 0) & (groups > 0))
    def _():
        solve(last - 1, 1)


def main_entry(recv, tab, out, *scratch):
    names = ("inbox", "whole", "index", "pos", "rows", "coefs", "results")
    sets = [dict(zip(names, scratch[3 + 7 * p : 10 + 7 * p])) for p in range(2)]
    main_kernel(recv, tab, out, *scratch[:3], sets, scratch[-1])


def main(recv, tab):
    entries = recv.shape[0] // 4
    devices = entries // CAP
    one_set = [
        pltpu.VMEM((32, BLOCK), jnp.float32),
        pltpu.VMEM((8, BLOCK), jnp.int32),
        pltpu.SMEM((8, BLOCK), jnp.int32),
        pltpu.VMEM((32, BLOCK), jnp.float32),
        pltpu.VMEM((GROUP * BLOCK, 2 * FIELDS), jnp.float32),
        pltpu.VMEM((8 * FIELDS, BLOCK), jnp.float32),
        pltpu.VMEM((8 * VARS, BLOCK), jnp.float32),
    ]
    return pl.pallas_call(
        main_entry,
        name="main",
        in_specs=[
            pl.BlockSpec(memory_space=pltpu.VMEM),
            pl.BlockSpec(memory_space=pl.ANY),
        ],
        out_specs=pl.BlockSpec(memory_space=pltpu.VMEM),
        out_shape=jax.ShapeDtypeStruct((entries * VARS, BLOCK), jnp.float32),
        scratch_shapes=[
            pltpu.VMEM((tab.shape[0] // ROOM, tab.shape[1]), jnp.float32),
            pltpu.VMEM((24, BLOCK), jnp.int32),
            pltpu.SMEM((24, BLOCK), jnp.int32),
            *one_set,
            *one_set,
            pltpu.SemaphoreType.DMA((4,)),
        ],
        compiler_params=pltpu.CompilerParams(vmem_limit_bytes=40 << 20),
        cost_estimate=pl.CostEstimate(flops=2 << 30, bytes_accessed=20 << 20, transcendentals=0),
    )(recv, tab)


PARTS = 4


def unpack_kernel(place_ref, answers, out_hbm, out_ref, sem):
    blocks = place_ref.shape[1]
    width = blocks * BLOCK // PARTS
    copies = []
    for b in range(blocks):
        out_ref[:, b * BLOCK : (b + 1) * BLOCK] = answers[pl.ds(place_ref[0, b], VARS), :]
        if (b + 1) * BLOCK % width == 0:
            part = pl.ds((b + 1) * BLOCK - width, width)
            copies.append(pltpu.make_async_copy(out_ref.at[:, part], out_hbm.at[:, part], sem.at[len(copies)]))
            copies[-1].start()
    for copy in copies:
        copy.wait()


def unpack(place, answers):
    blocks = place.shape[1]
    shape = (VARS, blocks * BLOCK)
    return pl.pallas_call(
        unpack_kernel,
        name="unpack",
        in_specs=[pl.BlockSpec(memory_space=pltpu.SMEM), pl.BlockSpec(memory_space=pltpu.VMEM)],
        out_specs=pl.BlockSpec(memory_space=pl.ANY),
        out_shape=jax.ShapeDtypeStruct(shape, jnp.float32),
        scratch_shapes=[pltpu.VMEM(shape, jnp.float32), pltpu.SemaphoreType.DMA((PARTS,))],
        compiler_params=pltpu.CompilerParams(vmem_limit_bytes=8 << 20),
    )(place, answers)


def per_device(recv_pos, donor_cell, block_owner, cell_geom, cell_values):
    devices = lax.axis_size(AXES)
    blocks = block_owner.shape[0]
    cells_per = cell_geom.shape[1]
    slots = devices * CAP
    swap = [(i, i ^ 1) for i in range(lax.axis_size("brick"))]
    geom_two = lax.ppermute(cell_geom, "brick", swap)
    vals_two = lax.ppermute(cell_values, "brick", swap)
    outgoing, place = pack(
        block_owner.reshape(1, blocks), recv_pos, donor_cell.reshape(blocks, BLOCK), cells_per, slots
    )
    arrived = lax.all_to_all(
        outgoing.reshape(devices, CAP, 4, BLOCK), AXES, split_axis=0, concat_axis=0, tiled=True
    )
    tab = table(cell_geom, cell_values, geom_two, vals_two)
    answer = main(arrived.reshape(slots * 4, BLOCK), tab)
    answers = lax.all_to_all(
        answer.reshape(devices, VARS, CAP, BLOCK), AXES, split_axis=0, concat_axis=0, tiled=True
    )
    return unpack(place, answers.reshape(slots * VARS, BLOCK))


def solution(mesh):
    placed = (
        P(None, AXES),
        P(AXES),
        P(AXES, None),
        P(None, AXES),
        P(None, AXES),
    )
    return jax.shard_map(
        per_device,
        mesh=mesh,
        in_specs=placed,
        out_specs=P(None, AXES),
        check_vma=False,
    )
```
